512 devices in a mesh: gx: 16 (over x, y_lo, core), gy: 16 (over z), gz: 2 (over y_hi).
Axes of the slice: x: 4, y: 4 (y_hi: 2, y_lo: 2; y = y_hi * 2 + y_lo), z: 16, core: 2. Of those that a mesh axis runs over, the one named last changes fastest.
Arguments:
- velocity: float32 [3, 32, 1536, 2048], P(None, 'gz', 'gy', 'gx'), may hold values from -6 to 6
- below: float32 [3, 2, 1536, 2048], P(None, None, 'gy', 'gx'), may hold values from -6 to 6
- above: float32 [3, 2, 1536, 2048], P(None, None, 'gy', 'gx'), may hold values from -6 to 6
- omega_x: int32 [2048, 256], P('gx'), may hold values from -1 to 1
- omega_y: int32 [1536, 256], P('gy'), may hold values from -1 to 1
- omega_z: int32 [32, 256], P('gz'), may hold values from -1 to 1
- phi_x: int32 [512, 2048], P(None, 'gx'), may hold values from -1 to 1
- phi_y: int32 [512, 1536], P(None, 'gy'), may hold values from -1 to 1
- phi_z: int32 [2, 32], P(None, 'gz'), may hold values from -1 to 1
Outputs:
- factor_x: float32 [2048, 256], P('gx')
- factor_y: float32 [1536, 256], P('gy')
- factor_z: float32 [32, 256], P('gz')
- core_sketch: float32 [512, 2, 512], P(('gx', 'gy', 'gz'))
The draws below stay inside these ranges and needn't reach their ends.
All inputs are finite; a program needn't handle non-finite values.
Results may differ from the reference program's by a relative error of at most 0.000088.
Values sent between devices are 32-bit elements; how exact they have to be, the bound alone decides.
No kernel may reach another device: no remote copies, remote signals or barrier semaphores. Data moves between devices by JAX's collectives and lax.ppermute only.
A program may use at most 64 MiB of HBM per device.

```python
import math
import jax
import jax.numpy as jnp
from jax import lax

R = 256
S = 512
CORE_C = 2
NX = 2048
NY = 1536
NZ = 32


def plant(result, key, low, top_value):
    spot = [jax.random.randint(jax.random.fold_in(key, axis), (), 0, length) for axis, length in enumerate(result.shape)]
    longest = result.shape.index(max(result.shape))
    beside = spot[:longest] + [(spot[longest] + 1) % result.shape[longest]] + spot[longest + 1:]
    return result.at[tuple(spot)].set(low).at[tuple(beside)].set(top_value)


def block_levels(rng, shape, shards, low, high):
    def one(dim, parts):
        draws = jax.random.uniform(jax.random.fold_in(jax.random.fold_in(rng, 6), dim), (parts,), jnp.float32, low / len(shards), high / len(shards))
        return jnp.repeat(jnp.exp(draws), shape[dim] // parts).reshape((-1,) + (1,) * (len(shape) - dim - 1))

    gain = one(*shards[0])
    for cut in shards[1:]:
        gain = gain * one(*cut)
    return gain


def noise(stream_key, dims, scale, bound, cuts=(), kind=jnp.bfloat16):
    array = scale * jax.random.normal(stream_key, dims, jnp.float32)
    if cuts:
        array = array * block_levels(stream_key, dims, cuts, -0.22, 0.18)
    return jnp.clip(array, -bound, bound).astype(kind)


def setup_inputs(seed: int = 0) -> dict:
    seeds = jax.random.split(jax.random.key(seed), 10)
    velocity = noise(seeds[0], (3, NZ, NY, NX), 1.0, 6.0, ((1, 2), (2, 16), (3, 16)), jnp.float32)
    below = noise(seeds[1], (3, 2, NY, NX), 1.0, 6.0, ((2, 16), (3, 16)), jnp.float32)
    above = noise(seeds[2], (3, 2, NY, NX), 1.0, 6.0, ((2, 16), (3, 16)), jnp.float32)
    omega_x = plant(jax.random.randint(seeds[3], (NX, R), -1, 2), jax.random.fold_in(seeds[3], 1), -1, 1).astype(jnp.int32)
    omega_y = plant(jax.random.randint(seeds[4], (NY, R), -1, 2), jax.random.fold_in(seeds[4], 1), -1, 1).astype(jnp.int32)
    omega_z = plant(jax.random.randint(seeds[5], (NZ, R), -1, 2), jax.random.fold_in(seeds[5], 1), -1, 1).astype(jnp.int32)
    phi_x = plant(jax.random.randint(seeds[6], (S, NX), -1, 2), jax.random.fold_in(seeds[6], 1), -1, 1).astype(jnp.int32)
    phi_y = plant(jax.random.randint(seeds[7], (S, NY), -1, 2), jax.random.fold_in(seeds[7], 1), -1, 1).astype(jnp.int32)
    phi_z = plant(jax.random.randint(seeds[8], (CORE_C, NZ), -1, 2), jax.random.fold_in(seeds[8], 1), -1, 1).astype(jnp.int32)
    return {"velocity": velocity, "below": below, "above": above, "omega_x": omega_x, "omega_y": omega_y, "omega_z": omega_z, "phi_x": phi_x, "phi_y": phi_y, "phi_z": phi_z}


precise = lax.Precision.HIGHEST

def derivative(padded, direction):
    length = padded.shape[direction] - 4

    def window(offset):
        return lax.slice_in_dim(padded, offset, offset + length, axis=direction)
    return (window(0) - 8.0 * window(1) + 8.0 * window(3) - window(4)) / 12.0

def criterion(gradient):
    summed = jnp.zeros(gradient[0].shape[1:], gradient[0].dtype)
    for component in range(3):
        for direction in range(3):
            summed = summed + gradient[direction][component] * gradient[component][direction]
    return -0.5 * summed

def reference(velocity, below, above, omega_x, omega_y, omega_z, phi_x, phi_y, phi_z):
    along_z = jnp.concatenate([below, velocity, above], axis=1)

    def plane(plane_index):
        stack = lax.dynamic_slice_in_dim(along_z, plane_index, 5, 1)
        middle = stack[:, 2:3]
        along_y = jnp.concatenate([middle[:, :, -2:], middle, middle[:, :, :2]], axis=2)
        along_x = jnp.concatenate([middle[:, :, :, -2:], middle, middle[:, :, :, :2]], axis=3)
        gradient = [derivative(along_x, 3), derivative(along_y, 2), derivative(stack, 1)]
        return criterion(gradient)[0]
    qfield = lax.map(plane, jnp.arange(NZ, dtype=jnp.int32))
    ternary_x = omega_x.astype(jnp.float32)
    ternary_y = omega_y.astype(jnp.float32)
    ternary_z = omega_z.astype(jnp.float32)
    contract_y = jnp.einsum('kji,jr->kir', qfield, ternary_y, precision=precise)
    factor_x = jnp.einsum('kir,kr->ir', contract_y, ternary_z, precision=precise) / math.sqrt(NY * NZ)
    contract_x = jnp.einsum('kji,ir->kjr', qfield, ternary_x, precision=precise)
    factor_y = jnp.einsum('kjr,kr->jr', contract_x, ternary_z, precision=precise) / math.sqrt(NX * NZ)
    factor_z = jnp.einsum('kjr,jr->kr', contract_x, ternary_y, precision=precise) / math.sqrt(NX * NY)
    sketch_x = phi_x.astype(jnp.float32)
    sketch_y = phi_y.astype(jnp.float32)
    sketch_z = phi_z.astype(jnp.float32)
    flattened = jnp.einsum('kji,ck->cji', qfield, sketch_z, precision=precise)
    leading = jnp.einsum('cji,ai->acj', flattened, sketch_x, precision=precise)
    core_sketch = jnp.einsum('acj,bj->acb', leading, sketch_y, precision=precise) / math.sqrt(NX * NY * NZ)
    return (factor_x, factor_y, factor_z, core_sketch)
```

```python
import math

import jax
import jax.numpy as jnp
from jax import lax
from jax.sharding import PartitionSpec as P


def shift_permute(cells, axis, step):
    count = lax.axis_size(axis)
    return lax.ppermute(cells, axis, [(i, (i + step) % count) for i in range(count)])


def extended(cells, axis, dim):
    length = cells.shape[dim]
    head = lax.slice_in_dim(cells, 0, 2, axis=dim)
    tail = lax.slice_in_dim(cells, length - 2, length, axis=dim)
    before = shift_permute(tail, axis, 1)
    after = shift_permute(head, axis, -1)
    return jnp.concatenate([before, cells, after], axis=dim)


def derivative(padded, direction):
    length = padded.shape[direction] - 4

    def window(offset):
        return lax.slice_in_dim(padded, offset, offset + length, axis=direction)

    return (window(0) - window(4)) + 8.0 * (window(3) - window(1))


def split(values):
    high = lax.reduce_precision(values, 8, 7)
    return high.astype(jnp.bfloat16), (values - high).astype(jnp.bfloat16)


def contract(spec, values, ternary):
    high, low = split(values)
    return jnp.einsum(spec, high, ternary, preferred_element_type=jnp.float32) + jnp.einsum(
        spec, low, ternary, preferred_element_type=jnp.float32
    )


def exchange(rows, axes):
    return lax.all_to_all(rows, axes, 0, 0, tiled=True)


def shards(velocity, below, above, omega_x, omega_y, omega_z, phi_x, phi_y, phi_z):
    total_x = 2048
    total_y = 1536
    total_z = 32
    gz = lax.axis_index("gz")
    near = jnp.where(gz == 0, velocity[:, 14:16], velocity[:, 0:2])
    far = shift_permute(near, "gz", 1)
    lower = jnp.where(gz == 0, below, far)
    upper = jnp.where(gz == 1, above, far)
    planes = jnp.concatenate([lower, velocity, upper], axis=1)
    grad = [
        derivative(extended(velocity, "gx", 3), 3),
        derivative(extended(velocity, "gy", 2), 2),
        derivative(planes, 1),
    ]
    diagonal = grad[0][0] * grad[0][0] + grad[1][1] * grad[1][1] + grad[2][2] * grad[2][2]
    mixed = grad[0][1] * grad[1][0] + grad[0][2] * grad[2][0] + grad[1][2] * grad[2][1]
    qfield = (-0.5 / 144.0) * (diagonal + 2.0 * mixed)

    wx = omega_x.astype(jnp.bfloat16)
    wy = omega_y.astype(jnp.bfloat16)
    wz = omega_z.astype(jnp.float32)
    contract_x = contract("kji,ir->kjr", qfield, wx)
    partial_y = jnp.sum(contract_x * wz[:, None, :], axis=0)
    partial_z = jnp.sum(contract_x * omega_y.astype(jnp.float32)[None], axis=1)
    flattened = jnp.einsum("kji,ck->cji", qfield, phi_z.astype(jnp.float32), precision=lax.Precision.HIGHEST)
    leading = contract("cji,ai->acj", flattened, phi_x.astype(jnp.bfloat16))
    leading = leading.reshape(16, 16, 2, 192).transpose(0, 2, 1, 3).reshape(32, 24, 128)
    factor_z_rows = jnp.broadcast_to(partial_z.reshape(16, 1, 2, 128), (16, 2, 2, 128)).reshape(32, 2, 128)
    send = jnp.concatenate([leading, partial_y.reshape(32, 6, 128), factor_z_rows], axis=1)
    got = exchange(send.reshape(1024, 128), ("gx", "gz")).reshape(16, 2, 32, 128)

    contract_y = contract("kji,jr->kir", qfield, wy)
    partial_x = jnp.sum(contract_y * wz[:, None, :], axis=0)

    summed = jnp.sum(got, axis=(0, 1))
    summed_z = jnp.sum(lax.dynamic_index_in_dim(got, gz, 1, keepdims=False)[:, 30:], axis=0)
    lead = summed[:24].reshape(16, 2, 96)
    core = contract("hcj,bj->hcb", lead, phi_y.astype(jnp.bfloat16)).reshape(16, 8, 128)
    send = jnp.concatenate(
        [core, partial_x.reshape(16, 16, 128), jnp.broadcast_to(summed_z[None], (16, 2, 128))], axis=1
    )
    got = jnp.sum(exchange(send.reshape(416, 128), "gy").reshape(16, 26, 128), axis=0)
    core_sketch = got[:8].reshape(1, 2, 512) * (1.0 / math.sqrt(total_x * total_y * total_z))
    other = shift_permute(got[8:24], "gz", 1)

    rows = jnp.concatenate([summed[24:30], got[24:26]], axis=0)
    got_y = exchange(jnp.broadcast_to(rows[None], (32, 8, 128)).reshape(256, 128), ("gx", "gz"))
    got_y = got_y.reshape(16, 2, 8, 128)
    factor_y = got_y[:, :, :6].reshape(96, 256) * (1.0 / math.sqrt(total_x * total_z))
    factor_z = lax.dynamic_index_in_dim(got_y, gz, 1, keepdims=False)[:, 6:].reshape(16, 256)
    factor_z = factor_z * (1.0 / math.sqrt(total_x * total_y))

    rows = got[8:24] + other
    got_x = exchange(jnp.broadcast_to(rows[None], (16, 16, 128)).reshape(256, 128), "gy")
    factor_x = got_x.reshape(128, 256) * (1.0 / math.sqrt(total_y * total_z))
    return (factor_x, factor_y, factor_z, core_sketch)


def solution(mesh):
    in_specs = (
        P(None, "gz", "gy", "gx"),
        P(None, None, "gy", "gx"),
        P(None, None, "gy", "gx"),
        P("gx", None),
        P("gy", None),
        P("gz", None),
        P(None, "gx"),
        P(None, "gy"),
        P(None, "gz"),
    )
    out_specs = (P("gx", None), P("gy", None), P("gz", None), P(("gx", "gy", "gz"), None, None))
    return jax.shard_map(shards, mesh=mesh, in_specs=in_specs, out_specs=out_specs, check_vma=False)
```

```python
import math

import jax
import jax.numpy as jnp
from jax import lax
from jax.experimental import pallas as pl
from jax.experimental.pallas import tpu as pltpu
from jax.sharding import PartitionSpec as P


def shift_permute(cells, axis, step):
    count = lax.axis_size(axis)
    return lax.ppermute(cells, axis, [(i, (i + step) % count) for i in range(count)])


def pack_kernel(vel, near, x_high, x_low, y_high, y_low):
    component = pl.program_id(0)
    gz = lax.axis_index("gz")
    lane = lax.broadcasted_iota(jnp.int32, (96, 128), 1)
    near[0] = vel[0, pl.ds(14 * (1 - gz), 2)]

    @pl.when(component == 0)
    def _():
        x_high[...] = jnp.zeros((96, 128), jnp.float32)
        x_low[...] = jnp.zeros((96, 128), jnp.float32)

    high = x_high[...]
    low = x_low[...]
    for k in range(16):
        spot = 2 * (16 * component + k)
        cells = vel[0, k]
        turned = pltpu.roll(cells, spot + 2, 1)
        high = jnp.where((lane >= spot) & (lane < spot + 2), turned, high)
        low = jnp.where((lane >= spot + 2) & (lane < spot + 4), turned, low)
        y_low[0, 2 * k : 2 * k + 2, :] = vel[0, k, 0:2, :]
        y_high[0, 2 * k : 2 * k + 2, :] = vel[0, k, 94:96, :]
    x_high[...] = high
    x_low[...] = low


def pack(velocity):
    rims = jax.ShapeDtypeStruct((96, 128), jnp.float32)
    rows = jax.ShapeDtypeStruct((3, 32, 128), jnp.float32)
    return pl.pallas_call(
        pack_kernel,
        grid=(3,),
        in_specs=[pl.BlockSpec((1, 16, 96, 128), lambda c: (c, 0, 0, 0))],
        out_specs=[
            pl.BlockSpec((1, 2, 96, 128), lambda c: (c, 0, 0, 0)),
            pl.BlockSpec((96, 128), lambda c: (0, 0)),
            pl.BlockSpec((96, 128), lambda c: (0, 0)),
            pl.BlockSpec((1, 32, 128), lambda c: (c, 0, 0)),
            pl.BlockSpec((1, 32, 128), lambda c: (c, 0, 0)),
        ],
        out_shape=[jax.ShapeDtypeStruct((3, 2, 96, 128), jnp.float32), rims, rims, rows, rows],
        name="pack_halos",
    )(velocity)


def field_kernel(
    phi_z, vel, far, below, above, x_left, x_right, y_before, y_after, wx, wy, wz, wyz, phx,
    send, part_x, padded, q_terms, flat, flat_terms, part_y, part_z, lead, sems,
):
    gz = lax.axis_index("gz")
    copies = [
        pltpu.make_async_copy(vel.at[c], padded.at[c, pl.ds(2, 16), pl.ds(8, 96), :], sems.at[c]) for c in range(3)
    ]
    for copy in copies:
        copy.start()

    def rims(lower, upper):
        pair = [
            pltpu.make_async_copy(lower, padded.at[:, pl.ds(0, 2), pl.ds(8, 96), :], sems.at[3]),
            pltpu.make_async_copy(upper, padded.at[:, pl.ds(18, 2), pl.ds(8, 96), :], sems.at[4]),
        ]
        for copy in pair:
            copy.start()
        for copy in pair:
            copy.wait()

    @pl.when(gz == 0)
    def _():
        rims(below, far)

    @pl.when(gz == 1)
    def _():
        rims(far, above)

    for copy in copies:
        copy.wait()
    for c in range(3):
        for k in range(16):
            padded[c, k + 2, 6:8, :] = y_before[c, 2 * k : 2 * k + 2, :]
            padded[c, k + 2, 104:106, :] = y_after[c, 2 * k : 2 * k + 2, :]
    flat[...] = jnp.zeros((256, 128), jnp.float32)
    part_y[...] = jnp.zeros((96, 256), jnp.float32)
    lane = lax.broadcasted_iota(jnp.int32, (16, 128), 1)

    def plane(k, carry):
        weight = [phi_z[c, k].astype(jnp.float32) for c in range(2)]
        for block in range(6):
            row = 16 * block
            at = row + 8
            along = [[], [], []]
            for c in range(3):
                spot = 2 * (16 * c + k)
                cells = padded[c, k + 2, at : at + 16, :]
                sides = jnp.where(lane < spot + 2, x_left[row : row + 16, :], x_right[row : row + 16, :])
                sides = pltpu.roll(sides, 126 - spot, 1)
                outer = pltpu.roll(jnp.where(lane >= 126, sides, cells), 2, 1) - pltpu.roll(
                    jnp.where(lane < 2, sides, cells), 126, 1
                )
                inner = pltpu.roll(jnp.where(lane < 1, sides, cells), 127, 1) - pltpu.roll(
                    jnp.where(lane >= 127, sides, cells), 1, 1
                )
                along[0].append(outer + 8.0 * inner)
                outer = padded[c, k + 2, at - 2 : at + 14, :] - padded[c, k + 2, at + 2 : at + 18, :]
                inner = padded[c, k + 2, at + 1 : at + 17, :] - padded[c, k + 2, at - 1 : at + 15, :]
                along[1].append(outer + 8.0 * inner)
                outer = padded[c, k, at : at + 16, :] - padded[c, k + 4, at : at + 16, :]
                inner = padded[c, k + 3, at : at + 16, :] - padded[c, k + 1, at : at + 16, :]
                along[2].append(outer + 8.0 * inner)
            diagonal = along[0][0] * along[0][0] + along[1][1] * along[1][1] + along[2][2] * along[2][2]
            mixed = along[0][1] * along[1][0] + along[0][2] * along[2][0] + along[1][2] * along[2][1]
            field = (-0.5 / 144.0) * (diagonal + 2.0 * mixed)
            high = field.astype(jnp.bfloat16)
            low = (field - high.astype(jnp.float32)).astype(jnp.bfloat16)
            place = pl.ds(pl.multiple_of(96 * k + row, 16), 16)
            q_terms[place, 0:128] = high
            q_terms[place, 128:256] = low
            for c in range(2):
                flat[96 * c + row : 96 * c + row + 16, :] += weight[c] * field
        return carry

    lax.fori_loop(0, 16, plane, 0)

    flat_high = flat[...].astype(jnp.bfloat16)
    flat_terms[:, 0:128] = flat_high
    flat_terms[:, 128:256] = (flat[...] - flat_high.astype(jnp.float32)).astype(jnp.bfloat16)
    lead[...] = lax.dot_general(
        phx[...], flat_terms[...], (((1,), (1,)), ((), ())), preferred_element_type=jnp.float32
    )
    lane8 = lax.broadcasted_iota(jnp.int32, (8, 128), 1)

    def products(k, carry):
        place = pl.ds(pl.multiple_of(96 * k, 96), 96)
        sums = jnp.dot(q_terms[place, :], wx[...], preferred_element_type=jnp.float32)
        part_y[...] += sums * wz[pl.ds(k, 1), :]
        part_z[pl.ds(k, 1), :] = jnp.sum(sums * wy[...], axis=0, keepdims=True)
        return carry

    lax.fori_loop(0, 16, products, 0)

    for chunk in range(32):
        base = 32 * chunk
        send[base : base + 16, :] = lead[16 * chunk : 16 * chunk + 16, 0:128]
        send[base + 16 : base + 24, :] = jnp.where(
            lane8 < 64,
            lead[16 * chunk : 16 * chunk + 8, 128:256],
            pltpu.roll(lead[16 * chunk + 8 : 16 * chunk + 16, 128:256], 64, 1),
        )
        for half in range(2):
            lanes = slice(128 * half, 128 * half + 128)
            send[base + 24 + 3 * half : base + 27 + 3 * half, :] = part_y[3 * chunk : 3 * chunk + 3, lanes]
            send[base + 30 + half : base + 31 + half, :] = part_z[chunk // 2 : chunk // 2 + 1, lanes]

    turned = jnp.dot(wyz[...], q_terms[...], preferred_element_type=jnp.float32)
    turned = turned[:, 0:128] + turned[:, 128:256]
    part_x[0] = turned[0:128, :].T
    part_x[1] = turned[128:256, :].T


def field(phi_z, velocity, far, below, above, sides, wx, wy, wz, wyz, phx):
    whole = pl.BlockSpec(memory_space=pltpu.VMEM)
    outside = pl.BlockSpec(memory_space=pl.ANY)
    return pl.pallas_call(
        field_kernel,
        in_specs=[pl.BlockSpec(memory_space=pltpu.SMEM)] + [outside] * 4 + [whole] * 9,
        out_specs=[whole] * 2,
        out_shape=[
            jax.ShapeDtypeStruct((1024, 128), jnp.float32),
            jax.ShapeDtypeStruct((2, 128, 128), jnp.float32),
        ],
        scratch_shapes=[
            pltpu.VMEM((3, 20, 112, 128), jnp.float32),
            pltpu.VMEM((1536, 256), jnp.bfloat16),
            pltpu.VMEM((256, 128), jnp.float32),
            pltpu.VMEM((256, 256), jnp.bfloat16),
            pltpu.VMEM((96, 256), jnp.float32),
            pltpu.VMEM((16, 256), jnp.float32),
            pltpu.VMEM((512, 256), jnp.float32),
            pltpu.SemaphoreType.DMA((5,)),
        ],
        compiler_params=pltpu.CompilerParams(vmem_limit_bytes=32 * 1024 * 1024),
        name="field_products",
    )(phi_z, velocity, far, below, above, *sides, wx, wy, wz, wyz, phx)


def split(values):
    high = lax.reduce_precision(values, 8, 7)
    return high.astype(jnp.bfloat16), (values - high).astype(jnp.bfloat16)


def exchange(rows, axes):
    return lax.all_to_all(rows, axes, 0, 0, tiled=True)


def shards(velocity, below, above, omega_x, omega_y, omega_z, phi_x, phi_y, phi_z):
    total_x = 2048
    total_y = 1536
    total_z = 32
    gz = lax.axis_index("gz")
    near, x_high, x_low, y_high, y_low = pack(velocity)
    far = shift_permute(near, "gz", 1)
    sides = [
        shift_permute(x_high, "gx", 1),
        shift_permute(x_low, "gx", -1),
        shift_permute(y_high, "gy", 1),
        shift_permute(y_low, "gy", -1),
    ]
    wx = omega_x.astype(jnp.bfloat16)
    wy = omega_y.astype(jnp.float32)
    wz = omega_z.astype(jnp.float32)
    wyz = (omega_z.T[:, :, None] * omega_y.T[:, None, :]).astype(jnp.bfloat16).reshape(256, 1536)
    phx = phi_x.reshape(16, 16, 2, 128).transpose(0, 2, 1, 3).reshape(512, 128).astype(jnp.bfloat16)
    send, part_x = field(
        phi_z, velocity, far, below, above, sides,
        jnp.concatenate([wx, wx], axis=0), wy, wz, wyz, jnp.concatenate([phx, phx], axis=1),
    )
    got = exchange(send, ("gx", "gz")).reshape(16, 2, 32, 128)
    mine = lax.dynamic_index_in_dim(part_x, gz, 0, keepdims=False)
    theirs = shift_permute(lax.dynamic_index_in_dim(part_x, 1 - gz, 0, keepdims=False), "gz", 1)
    part_x = mine + theirs

    summed = jnp.sum(got, axis=(0, 1))
    summed_z = jnp.sum(lax.dynamic_index_in_dim(got, gz, 1, keepdims=False)[:, 30:], axis=0)
    rest = jnp.concatenate([summed[16:24, :64], summed[16:24, 64:]], axis=0)
    lead_high, lead_low = split(jnp.concatenate([summed[:16], rest], axis=1))
    wide = phi_y.T.astype(jnp.bfloat16)
    none = jnp.zeros((96, 512), jnp.bfloat16)
    wide = jnp.concatenate(
        [jnp.concatenate([wide, none], axis=1), jnp.concatenate([none, wide], axis=1)], axis=0
    )
    core = jnp.dot(jnp.concatenate([lead_high, lead_low], axis=0), wide, preferred_element_type=jnp.float32)
    core = (core[:16] + core[16:]).reshape(16, 8, 128)
    send = jnp.concatenate(
        [core, part_x.reshape(16, 8, 128), jnp.broadcast_to(summed_z[None], (16, 2, 128))], axis=1
    )
    got = jnp.sum(exchange(send.reshape(288, 128), "gy").reshape(16, 18, 128), axis=0)
    core_sketch = got[:8].reshape(1, 2, 512) * (1.0 / math.sqrt(total_x * total_y * total_z))
    other = shift_permute(got[8:16], "gz", 1)

    rows = jnp.concatenate([summed[24:30], got[16:18]], axis=0)
    got_y = exchange(jnp.broadcast_to(rows[None], (32, 8, 128)).reshape(256, 128), ("gx", "gz"))
    got_y = got_y.reshape(16, 2, 8, 128)
    factor_y = got_y[:, :, :6].reshape(32, 2, 3, 128).transpose(0, 2, 1, 3).reshape(96, 256)
    factor_y = factor_y * (1.0 / math.sqrt(total_x * total_z))
    factor_z = lax.dynamic_index_in_dim(got_y, gz, 1, keepdims=False)[:, 6:].reshape(16, 256)
    factor_z = factor_z * (1.0 / math.sqrt(total_x * total_y))

    first = jnp.where(gz == 0, got[8:16], other)
    second = jnp.where(gz == 0, other, got[8:16])
    rows = jnp.concatenate([first, second], axis=0)
    got_x = exchange(jnp.broadcast_to(rows[None], (16, 16, 128)).reshape(256, 128), "gy")
    factor_x = got_x.reshape(16, 2, 8, 128).transpose(0, 2, 1, 3).reshape(128, 256)
    factor_x = factor_x * (1.0 / math.sqrt(total_y * total_z))
    return (factor_x, factor_y, factor_z, core_sketch)


def solution(mesh):
    in_specs = (
        P(None, "gz", "gy", "gx"),
        P(None, None, "gy", "gx"),
        P(None, None, "gy", "gx"),
        P("gx", None),
        P("gy", None),
        P("gz", None),
        P(None, "gx"),
        P(None, "gy"),
        P(None, "gz"),
    )
    out_specs = (P("gx", None), P("gy", None), P("gz", None), P(("gx", "gy", "gz"), None, None))
    return jax.shard_map(shards, mesh=mesh, in_specs=in_specs, out_specs=out_specs, check_vma=False)
```

```python
import math

import jax
import jax.numpy as jnp
from jax import lax
from jax.experimental import pallas as pl
from jax.experimental.pallas import tpu as pltpu
from jax.sharding import PartitionSpec as P


def shift_permute(cells, axis, step):
    count = lax.axis_size(axis)
    return lax.ppermute(cells, axis, [(i, (i + step) % count) for i in range(count)])


def pack_kernel(vel, near, x_high, x_low, y_high, y_low, held, sems):
    gz = lax.axis_index("gz")
    copies = [
        pltpu.make_async_copy(
            vel.at[part // 2, pl.ds(8 * (part % 2), 8)], held.at[part // 2, pl.ds(8 * (part % 2), 8)], sems.at[part]
        )
        for part in range(6)
    ]
    for copy in copies:
        copy.start()
    lane = lax.broadcasted_iota(jnp.int32, (96, 128), 1)
    high = jnp.zeros((96, 128), jnp.float32)
    low = jnp.zeros((96, 128), jnp.float32)
    rims = []
    for part in range(6):
        copies[part].wait()
        c = part // 2
        if part % 2 == 1:
            rims.append(
                pltpu.make_async_copy(held.at[c, pl.ds(14 * (1 - gz), 2)], near.at[c], sems.at[6 + c])
            )
            rims[-1].start()
        for k in range(8 * (part % 2), 8 * (part % 2) + 8):
            spot = 2 * (16 * c + k)
            turned = pltpu.roll(held[c, k], spot + 2, 1)
            high = jnp.where((lane >= spot) & (lane < spot + 2), turned, high)
            low = jnp.where((lane >= spot + 2) & (lane < spot + 4), turned, low)
            y_low[c, 2 * k : 2 * k + 2, :] = held[c, k, 0:2, :]
            y_high[c, 2 * k : 2 * k + 2, :] = held[c, k, 94:96, :]
    x_high[...] = high
    x_low[...] = low
    for rim in rims:
        rim.wait()


def pack(velocity):
    rims = jax.ShapeDtypeStruct((96, 128), jnp.float32)
    rows = jax.ShapeDtypeStruct((3, 32, 128), jnp.float32)
    whole = pl.BlockSpec(memory_space=pltpu.VMEM)
    outside = pl.BlockSpec(memory_space=pl.ANY)
    return pl.pallas_call(
        pack_kernel,
        in_specs=[outside],
        out_specs=[outside] + [whole] * 4,
        out_shape=[jax.ShapeDtypeStruct((3, 2, 96, 128), jnp.float32), rims, rims, rows, rows],
        scratch_shapes=[pltpu.VMEM((3, 16, 96, 128), jnp.float32), pltpu.SemaphoreType.DMA((9,))],
        compiler_params=pltpu.CompilerParams(vmem_limit_bytes=60 * 1024 * 1024),
        name="pack_halos",
    )(velocity)


def field_kernel(
    phi_z, vel, far, below, above, x_left, x_right, y_before, y_after, omega_x, omega_y, omega_z, phi_x,
    send, mine, theirs,
    padded, sides, x_held, y_held, wx_held, wy_held, wz_held, px_held,
    q_terms, flat, flat_terms, wx, wyz, phx, part_y, part_z, lead, sems,
):
    gz = lax.axis_index("gz")
    middle = pl.ds(8, 96)
    x_copies = [
        pltpu.make_async_copy(x_left, x_held.at[0], sems.at[0]),
        pltpu.make_async_copy(x_right, x_held.at[1], sems.at[1]),
    ]
    y_copies = [
        pltpu.make_async_copy(y_before, y_held.at[0], sems.at[2]),
        pltpu.make_async_copy(y_after, y_held.at[1], sems.at[3]),
    ]
    cells_copies = [
        pltpu.make_async_copy(vel.at[c], padded.at[c, pl.ds(2, 16), middle, :], sems.at[4 + c]) for c in range(3)
    ]
    far_low = pltpu.make_async_copy(far, padded.at[:, pl.ds(0, 2), middle, :], sems.at[7])
    far_high = pltpu.make_async_copy(far, padded.at[:, pl.ds(18, 2), middle, :], sems.at[8])
    rim_low = pltpu.make_async_copy(below, padded.at[:, pl.ds(0, 2), middle, :], sems.at[7])
    rim_high = pltpu.make_async_copy(above, padded.at[:, pl.ds(18, 2), middle, :], sems.at[8])
    weight_copies = [
        pltpu.make_async_copy(omega_x, wx_held, sems.at[9]),
        pltpu.make_async_copy(omega_y, wy_held, sems.at[10]),
        pltpu.make_async_copy(omega_z, wz_held, sems.at[11]),
        pltpu.make_async_copy(phi_x, px_held, sems.at[12]),
    ]
    for copy in x_copies + cells_copies + y_copies:
        copy.start()

    @pl.when(gz == 0)
    def _():
        rim_low.start()
        far_high.start()

    @pl.when(gz == 1)
    def _():
        far_low.start()
        rim_high.start()

    for copy in weight_copies:
        copy.start()
    for copy in x_copies:
        copy.wait()

    lane_all = lax.broadcasted_iota(jnp.int32, (96, 128), 1)

    def place(k, carry):
        for c in range(3):
            spot = 2 * (16 * c + k)
            both = jnp.where(lane_all < spot + 2, x_held[0], x_held[1])
            sides[c, k] = pltpu.roll(both, 126 - spot, 1)
        return carry

    lax.fori_loop(0, 16, place, 0, unroll=2)

    for copy in y_copies + cells_copies:
        copy.wait()
    for c in range(3):
        for k in range(16):
            padded[c, k + 2, 6:8, :] = y_held[0, c, 2 * k : 2 * k + 2, :]
            padded[c, k + 2, 104:106, :] = y_held[1, c, 2 * k : 2 * k + 2, :]
    flat[...] = jnp.zeros((256, 128), jnp.float32)

    @pl.when(gz == 0)
    def _():
        rim_low.wait()
        far_high.wait()

    @pl.when(gz == 1)
    def _():
        far_low.wait()
        rim_high.wait()

    lane = lax.broadcasted_iota(jnp.int32, (16, 128), 1)

    def plane(k, carry):
        weight = [phi_z[c, k].astype(jnp.float32) for c in range(2)]
        for block in range(6):
            row = 16 * block
            at = row + 8
            along = [[], [], []]
            for c in range(3):
                cells = padded[c, k + 2, at : at + 16, :]
                rim = sides[c, k, row : row + 16, :]
                outer = pltpu.roll(jnp.where(lane >= 126, rim, cells), 2, 1) - pltpu.roll(
                    jnp.where(lane < 2, rim, cells), 126, 1
                )
                inner = pltpu.roll(jnp.where(lane < 1, rim, cells), 127, 1) - pltpu.roll(
                    jnp.where(lane >= 127, rim, cells), 1, 1
                )
                along[0].append(outer + 8.0 * inner)
                outer = padded[c, k + 2, at - 2 : at + 14, :] - padded[c, k + 2, at + 2 : at + 18, :]
                inner = padded[c, k + 2, at + 1 : at + 17, :] - padded[c, k + 2, at - 1 : at + 15, :]
                along[1].append(outer + 8.0 * inner)
                outer = padded[c, k, at : at + 16, :] - padded[c, k + 4, at : at + 16, :]
                inner = padded[c, k + 3, at : at + 16, :] - padded[c, k + 1, at : at + 16, :]
                along[2].append(outer + 8.0 * inner)
            diagonal = along[0][0] * along[0][0] + along[1][1] * along[1][1] + along[2][2] * along[2][2]
            mixed = along[0][1] * along[1][0] + along[0][2] * along[2][0] + along[1][2] * along[2][1]
            field = (-0.5 / 144.0) * (diagonal + 2.0 * mixed)
            high = field.astype(jnp.bfloat16)
            low = (field - high.astype(jnp.float32)).astype(jnp.bfloat16)
            rows = pl.ds(pl.multiple_of(96 * k + row, 16), 16)
            q_terms[rows, 0:128] = high
            q_terms[rows, 128:256] = low
            for c in range(2):
                flat[96 * c + row : 96 * c + row + 16, :] += weight[c] * field
        return carry

    lax.fori_loop(0, 16, plane, 0, unroll=2)

    for copy in weight_copies:
        copy.wait()
    wx[0:128, :] = wx_held[...].astype(jnp.float32).astype(jnp.bfloat16)
    wx[128:256, :] = wx_held[...].astype(jnp.float32).astype(jnp.bfloat16)
    phx[:, 0:128] = px_held[...].astype(jnp.float32).astype(jnp.bfloat16)
    phx[:, 128:256] = px_held[...].astype(jnp.float32).astype(jnp.bfloat16)
    wy = wy_held[...].astype(jnp.float32)
    wz = wz_held[...].astype(jnp.float32)

    flat_high = flat[...].astype(jnp.bfloat16)
    flat_terms[:, 0:128] = flat_high
    flat_terms[:, 128:256] = (flat[...] - flat_high.astype(jnp.float32)).astype(jnp.bfloat16)
    leading = lax.dot_general(
        phx[...], flat_terms[...], (((1,), (1,)), ((), ())), preferred_element_type=jnp.float32
    )
    lead[0] = leading[:, 0:128]
    lead[1] = leading[:, 128:256]

    total_y = jnp.zeros((96, 256), jnp.float32)
    for k in range(16):
        rows = slice(96 * k, 96 * k + 96)
        sums = jnp.dot(q_terms[rows, :], wx[...], preferred_element_type=jnp.float32)
        total_y = total_y + sums * wz[k : k + 1, :]
        part_z[k : k + 1, :] = jnp.sum(sums * wy, axis=0, keepdims=True)
        wyz[rows, :] = (wy * wz[k : k + 1, :]).astype(jnp.bfloat16)
    part_y[...] = total_y

    lane8 = lax.broadcasted_iota(jnp.int32, (8, 128), 1)
    for g in range(16):
        for z in range(2):
            base = 40 * (2 * g + z)
            near = 32 * g + z
            send[base : base + 16, :] = lead[0, pl.ds(near, 16, stride=2), :]
            send[base + 16 : base + 24, :] = jnp.where(
                lane8 < 64,
                lead[1, pl.ds(near, 8, stride=2), :],
                pltpu.roll(lead[1, pl.ds(near + 16, 8, stride=2), :], 64, 1),
            )
            for half in range(2):
                lanes = slice(128 * half, 128 * half + 128)
                send[base + 24 + 6 * half : base + 30 + 6 * half, :] = part_y[6 * g : 6 * g + 6, lanes]
                send[base + 36 + half : base + 37 + half, :] = part_z[g : g + 1, lanes]
            send[base + 38 : base + 40, :] = jnp.zeros((2, 128), jnp.float32)

    turned = lax.dot_general(
        q_terms[...], wyz[...], (((0,), (0,)), ((), ())), preferred_element_type=jnp.float32
    )
    turned = turned[0:128, :] + turned[128:256, :]
    mine[...] = jnp.where(gz == 0, turned[:, 0:128], turned[:, 128:256])
    theirs[...] = jnp.where(gz == 0, turned[:, 128:256], turned[:, 0:128])


def field(phi_z, velocity, far, below, above, sides, omega_x, omega_y, omega_z, phi_x):
    whole = pl.BlockSpec(memory_space=pltpu.VMEM)
    outside = pl.BlockSpec(memory_space=pl.ANY)
    half = jax.ShapeDtypeStruct((128, 128), jnp.float32)
    return pl.pallas_call(
        field_kernel,
        in_specs=[pl.BlockSpec(memory_space=pltpu.SMEM)] + [outside] * 12,
        out_specs=[whole] * 3,
        out_shape=[jax.ShapeDtypeStruct((1280, 128), jnp.float32), half, half],
        scratch_shapes=[
            pltpu.VMEM((3, 20, 112, 128), jnp.float32),
            pltpu.VMEM((3, 16, 96, 128), jnp.float32),
            pltpu.VMEM((2, 96, 128), jnp.float32),
            pltpu.VMEM((2, 3, 32, 128), jnp.float32),
            pltpu.VMEM((128, 256), jnp.int32),
            pltpu.VMEM((96, 256), jnp.int32),
            pltpu.VMEM((16, 256), jnp.int32),
            pltpu.VMEM((512, 128), jnp.int32),
            pltpu.VMEM((1536, 256), jnp.bfloat16),
            pltpu.VMEM((256, 128), jnp.float32),
            pltpu.VMEM((256, 256), jnp.bfloat16),
            pltpu.VMEM((256, 256), jnp.bfloat16),
            pltpu.VMEM((1536, 256), jnp.bfloat16),
            pltpu.VMEM((512, 256), jnp.bfloat16),
            pltpu.VMEM((96, 256), jnp.float32),
            pltpu.VMEM((16, 256), jnp.float32),
            pltpu.VMEM((2, 512, 128), jnp.float32),
            pltpu.SemaphoreType.DMA((13,)),
        ],
        compiler_params=pltpu.CompilerParams(vmem_limit_bytes=60 * 1024 * 1024),
        name="field_products",
    )(phi_z, velocity, far, below, above, *sides, omega_x, omega_y, omega_z, phi_x)


def split(values):
    high = lax.reduce_precision(values, 8, 7)
    return high.astype(jnp.bfloat16), (values - high).astype(jnp.bfloat16)


def exchange(rows, axes):
    return lax.all_to_all(rows, axes, 0, 0, tiled=True)


def shards(velocity, below, above, omega_x, omega_y, omega_z, phi_x, phi_y, phi_z):
    total_x = 2048
    total_y = 1536
    total_z = 32
    gz = lax.axis_index("gz")
    near, x_high, x_low, y_high, y_low = pack(velocity)
    far = shift_permute(near, "gz", 1)
    sides = [
        shift_permute(x_high, "gx", 1),
        shift_permute(x_low, "gx", -1),
        shift_permute(y_high, "gy", 1),
        shift_permute(y_low, "gy", -1),
    ]
    send, mine, theirs = field(phi_z, velocity, far, below, above, sides, omega_x, omega_y, omega_z, phi_x)
    got = exchange(send, ("gx", "gz")).reshape(16, 2, 40, 128)
    part_x = mine + shift_permute(theirs, "gz", 1)

    summed = jnp.sum(got, axis=(0, 1))
    summed_z = jnp.sum(lax.dynamic_index_in_dim(got, gz, 1, keepdims=False)[:, 36:38], axis=0)
    rest = jnp.concatenate([summed[16:24, :64], summed[16:24, 64:]], axis=0)
    lead_high, lead_low = split(jnp.concatenate([summed[:16], rest], axis=1))
    wide = phi_y.T.astype(jnp.bfloat16)
    none = jnp.zeros((96, 512), jnp.bfloat16)
    wide = jnp.concatenate(
        [jnp.concatenate([wide, none], axis=1), jnp.concatenate([none, wide], axis=1)], axis=0
    )
    core = jnp.dot(jnp.concatenate([lead_high, lead_low], axis=0), wide, preferred_element_type=jnp.float32)
    core = (core[:16] + core[16:]).reshape(16, 8, 128)
    send = jnp.concatenate(
        [core, part_x.reshape(16, 8, 128), jnp.broadcast_to(summed_z[None], (16, 2, 128))], axis=1
    )
    got = jnp.sum(exchange(send.reshape(288, 128), "gy").reshape(16, 18, 128), axis=0)
    core_sketch = got[:8].reshape(1, 2, 512) * (1.0 / math.sqrt(total_x * total_y * total_z))

    got_y = lax.all_gather(summed[24:40], "gx", axis=0, tiled=True).reshape(16, 16, 128)
    factor_y = got_y[:, :12].reshape(16, 2, 6, 128).transpose(0, 2, 1, 3).reshape(96, 256)
    factor_y = factor_y * (1.0 / math.sqrt(total_x * total_z))

    got_z = lax.all_gather(got[16:18], "gx", axis=0, tiled=True)
    factor_z = got_z.reshape(16, 256) * (1.0 / math.sqrt(total_x * total_y))

    got_x = exchange(jnp.broadcast_to(got[None, 8:16], (32, 8, 128)).reshape(256, 128), ("gy", "gz"))
    factor_x = got_x.reshape(16, 2, 8, 128).transpose(0, 2, 1, 3).reshape(128, 256)
    factor_x = factor_x * (1.0 / math.sqrt(total_y * total_z))
    return (factor_x, factor_y, factor_z, core_sketch)


def solution(mesh):
    in_specs = (
        P(None, "gz", "gy", "gx"),
        P(None, None, "gy", "gx"),
        P(None, None, "gy", "gx"),
        P("gx", None),
        P("gy", None),
        P("gz", None),
        P(None, "gx"),
        P(None, "gy"),
        P(None, "gz"),
    )
    out_specs = (P("gx", None), P("gy", None), P("gz", None), P(("gx", "gy", "gz"), None, None))
    return jax.shard_map(shards, mesh=mesh, in_specs=in_specs, out_specs=out_specs, check_vma=False)
```

```python
import math

import jax
import jax.numpy as jnp
from jax import lax
from jax.experimental import pallas as pl
from jax.experimental.pallas import tpu as pltpu
from jax.sharding import PartitionSpec as P


def shift_permute(cells, axis, step):
    count = lax.axis_size(axis)
    return lax.ppermute(cells, axis, [(i, (i + step) % count) for i in range(count)])


def pack_kernel(vel, near, x_high, x_low, y_high, y_low, held, sems):
    gz = lax.axis_index("gz")
    copies = [
        pltpu.make_async_copy(
            vel.at[part // 2, pl.ds(8 * (part % 2), 8)], held.at[part // 2, pl.ds(8 * (part % 2), 8)], sems.at[part]
        )
        for part in range(6)
    ]
    for copy in copies:
        copy.start()
    lane = lax.broadcasted_iota(jnp.int32, (96, 128), 1)
    high = jnp.zeros((96, 128), jnp.float32)
    low = jnp.zeros((96, 128), jnp.float32)
    rims = []
    for part in range(6):
        copies[part].wait()
        c = part // 2
        if part % 2 == 1:
            rims.append(
                pltpu.make_async_copy(held.at[c, pl.ds(14 * (1 - gz), 2)], near.at[c], sems.at[6 + c])
            )
            rims[-1].start()
        for k in range(8 * (part % 2), 8 * (part % 2) + 8):
            spot = 2 * (16 * c + k)
            turned = pltpu.roll(held[c, k], spot + 2, 1)
            high = jnp.where((lane >= spot) & (lane < spot + 2), turned, high)
            low = jnp.where((lane >= spot + 2) & (lane < spot + 4), turned, low)
            y_low[c, 2 * k : 2 * k + 2, :] = held[c, k, 0:2, :]
            y_high[c, 2 * k : 2 * k + 2, :] = held[c, k, 94:96, :]
    x_high[...] = high
    x_low[...] = low
    for rim in rims:
        rim.wait()


def pack(velocity):
    rims = jax.ShapeDtypeStruct((96, 128), jnp.float32)
    rows = jax.ShapeDtypeStruct((3, 32, 128), jnp.float32)
    whole = pl.BlockSpec(memory_space=pltpu.VMEM)
    outside = pl.BlockSpec(memory_space=pl.ANY)
    return pl.pallas_call(
        pack_kernel,
        in_specs=[outside],
        out_specs=[outside] + [whole] * 4,
        out_shape=[jax.ShapeDtypeStruct((3, 2, 96, 128), jnp.float32), rims, rims, rows, rows],
        scratch_shapes=[pltpu.VMEM((3, 16, 96, 128), jnp.float32), pltpu.SemaphoreType.DMA((9,))],
        compiler_params=pltpu.CompilerParams(vmem_limit_bytes=60 * 1024 * 1024),
        name="pack_halos",
    )(velocity)


def field_kernel(
    vel, far, below, above, x_left, x_right, y_before, y_after, omega_x, omega_y, omega_z, phi_x, phi_z,
    send, mine, theirs,
    padded, sides, x_held, y_held, wx_held, wy_held, wz_held, px_held,
    q_terms, flat, flat_terms, wx, wyz, phx, part_y, part_z, lead, pz_held, sems,
):
    gz = lax.axis_index("gz")
    middle = pl.ds(8, 96)
    x_copies = [
        pltpu.make_async_copy(x_left, x_held.at[0], sems.at[0]),
        pltpu.make_async_copy(x_right, x_held.at[1], sems.at[1]),
    ]
    y_copies = [
        pltpu.make_async_copy(y_before, y_held.at[0], sems.at[2]),
        pltpu.make_async_copy(y_after, y_held.at[1], sems.at[3]),
    ]
    cells_copies = [
        pltpu.make_async_copy(vel.at[c], padded.at[c, pl.ds(2, 16), middle, :], sems.at[4 + c]) for c in range(3)
    ]
    far_low = pltpu.make_async_copy(far, padded.at[:, pl.ds(0, 2), middle, :], sems.at[7])
    far_high = pltpu.make_async_copy(far, padded.at[:, pl.ds(18, 2), middle, :], sems.at[8])
    rim_low = pltpu.make_async_copy(below, padded.at[:, pl.ds(0, 2), middle, :], sems.at[7])
    rim_high = pltpu.make_async_copy(above, padded.at[:, pl.ds(18, 2), middle, :], sems.at[8])
    weight_copies = [
        pltpu.make_async_copy(omega_x, wx_held, sems.at[9]),
        pltpu.make_async_copy(omega_y, wy_held, sems.at[10]),
        pltpu.make_async_copy(omega_z, wz_held, sems.at[11]),
        pltpu.make_async_copy(phi_x, px_held, sems.at[12]),
    ]
    z_copy = pltpu.make_async_copy(phi_z, pz_held, sems.at[13])
    for copy in x_copies + cells_copies + y_copies + [z_copy]:
        copy.start()

    @pl.when(gz == 0)
    def _():
        rim_low.start()
        far_high.start()

    @pl.when(gz == 1)
    def _():
        far_low.start()
        rim_high.start()

    for copy in weight_copies:
        copy.start()
    for copy in x_copies:
        copy.wait()

    lane_all = lax.broadcasted_iota(jnp.int32, (96, 128), 1)

    def place(k, carry):
        for c in range(3):
            spot = 2 * (16 * c + k)
            both = jnp.where(lane_all < spot + 2, x_held[0], x_held[1])
            sides[c, k] = pltpu.roll(both, 126 - spot, 1)
        return carry

    lax.fori_loop(0, 16, place, 0, unroll=2)

    for copy in y_copies + cells_copies + [z_copy]:
        copy.wait()
    for c in range(3):
        for k in range(16):
            padded[c, k + 2, 6:8, :] = y_held[0, c, 2 * k : 2 * k + 2, :]
            padded[c, k + 2, 104:106, :] = y_held[1, c, 2 * k : 2 * k + 2, :]
    flat[...] = jnp.zeros((256, 128), jnp.float32)

    @pl.when(gz == 0)
    def _():
        rim_low.wait()
        far_high.wait()

    @pl.when(gz == 1)
    def _():
        far_low.wait()
        rim_high.wait()

    lane = lax.broadcasted_iota(jnp.int32, (16, 128), 1)

    def plane(k, carry):
        weight = [pz_held[c, k].astype(jnp.float32) for c in range(2)]
        for block in range(6):
            row = 16 * block
            at = row + 8
            along = [[], [], []]
            for c in range(3):
                cells = padded[c, k + 2, at : at + 16, :]
                rim = sides[c, k, row : row + 16, :]
                outer = pltpu.roll(jnp.where(lane >= 126, rim, cells), 2, 1) - pltpu.roll(
                    jnp.where(lane < 2, rim, cells), 126, 1
                )
                inner = pltpu.roll(jnp.where(lane < 1, rim, cells), 127, 1) - pltpu.roll(
                    jnp.where(lane >= 127, rim, cells), 1, 1
                )
                along[0].append(outer + 8.0 * inner)
                outer = padded[c, k + 2, at - 2 : at + 14, :] - padded[c, k + 2, at + 2 : at + 18, :]
                inner = padded[c, k + 2, at + 1 : at + 17, :] - padded[c, k + 2, at - 1 : at + 15, :]
                along[1].append(outer + 8.0 * inner)
                outer = padded[c, k, at : at + 16, :] - padded[c, k + 4, at : at + 16, :]
                inner = padded[c, k + 3, at : at + 16, :] - padded[c, k + 1, at : at + 16, :]
                along[2].append(outer + 8.0 * inner)
            diagonal = along[0][0] * along[0][0] + along[1][1] * along[1][1] + along[2][2] * along[2][2]
            mixed = along[0][1] * along[1][0] + along[0][2] * along[2][0] + along[1][2] * along[2][1]
            field = (-0.5 / 144.0) * (diagonal + 2.0 * mixed)
            high = field.astype(jnp.bfloat16)
            low = (field - high.astype(jnp.float32)).astype(jnp.bfloat16)
            rows = pl.ds(pl.multiple_of(96 * k + row, 16), 16)
            q_terms[rows, 0:128] = high
            q_terms[rows, 128:256] = low
            for c in range(2):
                flat[96 * c + row : 96 * c + row + 16, :] += weight[c] * field
        return carry

    lax.fori_loop(0, 16, plane, 0, unroll=4)

    for copy in weight_copies:
        copy.wait()
    wx[0:128, :] = wx_held[...].astype(jnp.float32).astype(jnp.bfloat16)
    wx[128:256, :] = wx_held[...].astype(jnp.float32).astype(jnp.bfloat16)
    phx[:, 0:128] = px_held[...].astype(jnp.float32).astype(jnp.bfloat16)
    phx[:, 128:256] = px_held[...].astype(jnp.float32).astype(jnp.bfloat16)
    wy = wy_held[...].astype(jnp.float32)
    wz = wz_held[...].astype(jnp.float32)

    flat_high = flat[...].astype(jnp.bfloat16)
    flat_terms[:, 0:128] = flat_high
    flat_terms[:, 128:256] = (flat[...] - flat_high.astype(jnp.float32)).astype(jnp.bfloat16)
    leading = lax.dot_general(
        phx[...], flat_terms[...], (((1,), (1,)), ((), ())), preferred_element_type=jnp.float32
    )
    lead[0] = leading[:, 0:128]
    lead[1] = leading[:, 128:256]

    total_y = jnp.zeros((96, 256), jnp.float32)
    for k in range(16):
        rows = slice(96 * k, 96 * k + 96)
        sums = jnp.dot(q_terms[rows, :], wx[...], preferred_element_type=jnp.float32)
        total_y = total_y + sums * wz[k : k + 1, :]
        part_z[k : k + 1, :] = jnp.sum(sums * wy, axis=0, keepdims=True)
        wyz[rows, :] = (wy * wz[k : k + 1, :]).astype(jnp.bfloat16)
    part_y[...] = total_y

    lane8 = lax.broadcasted_iota(jnp.int32, (8, 128), 1)
    shares = [part_z[pl.ds(pl.multiple_of(8 * jnp.abs(z - gz), 8), 8), :] for z in range(2)]
    for g in range(16):
        for z in range(2):
            base = 52 * (2 * g + z)
            near = 32 * g + z
            send[base : base + 16, :] = lead[0, pl.ds(near, 16, stride=2), :]
            send[base + 16 : base + 24, :] = jnp.where(
                lane8 < 64,
                lead[1, pl.ds(near, 8, stride=2), :],
                pltpu.roll(lead[1, pl.ds(near + 16, 8, stride=2), :], 64, 1),
            )
            for half in range(2):
                lanes = slice(128 * half, 128 * half + 128)
                send[base + 24 + 8 * half : base + 32 + 8 * half, :] = shares[z][:, lanes]
                send[base + 40 + 6 * half : base + 46 + 6 * half, :] = part_y[6 * g : 6 * g + 6, lanes]

    turned = lax.dot_general(
        q_terms[...], wyz[...], (((0,), (0,)), ((), ())), preferred_element_type=jnp.float32
    )
    turned = turned[0:128, :] + turned[128:256, :]
    mine[...] = jnp.where(gz == 0, turned[:, 0:128], turned[:, 128:256])
    theirs[...] = jnp.where(gz == 0, turned[:, 128:256], turned[:, 0:128])


def field(velocity, far, below, above, sides, omega_x, omega_y, omega_z, phi_x, phi_z):
    whole = pl.BlockSpec(memory_space=pltpu.VMEM)
    outside = pl.BlockSpec(memory_space=pl.ANY)
    half = jax.ShapeDtypeStruct((128, 128), jnp.float32)
    return pl.pallas_call(
        field_kernel,
        in_specs=[outside] * 13,
        out_specs=[whole] * 3,
        out_shape=[jax.ShapeDtypeStruct((1664, 128), jnp.float32), half, half],
        scratch_shapes=[
            pltpu.VMEM((3, 20, 112, 128), jnp.float32),
            pltpu.VMEM((3, 16, 96, 128), jnp.float32),
            pltpu.VMEM((2, 96, 128), jnp.float32),
            pltpu.VMEM((2, 3, 32, 128), jnp.float32),
            pltpu.VMEM((128, 256), jnp.int32),
            pltpu.VMEM((96, 256), jnp.int32),
            pltpu.VMEM((16, 256), jnp.int32),
            pltpu.VMEM((512, 128), jnp.int32),
            pltpu.VMEM((1536, 256), jnp.bfloat16),
            pltpu.VMEM((256, 128), jnp.float32),
            pltpu.VMEM((256, 256), jnp.bfloat16),
            pltpu.VMEM((256, 256), jnp.bfloat16),
            pltpu.VMEM((1536, 256), jnp.bfloat16),
            pltpu.VMEM((512, 256), jnp.bfloat16),
            pltpu.VMEM((96, 256), jnp.float32),
            pltpu.VMEM((16, 256), jnp.float32),
            pltpu.VMEM((2, 512, 128), jnp.float32),
            pltpu.SMEM((2, 16), jnp.int32),
            pltpu.SemaphoreType.DMA((14,)),
        ],
        compiler_params=pltpu.CompilerParams(vmem_limit_bytes=60 * 1024 * 1024),
        name="field_products",
    )(velocity, far, below, above, *sides, omega_x, omega_y, omega_z, phi_x, phi_z)


def split(values):
    high = lax.reduce_precision(values, 8, 7)
    return high.astype(jnp.bfloat16), (values - high).astype(jnp.bfloat16)


def exchange(rows, axes):
    return lax.all_to_all(rows, axes, 0, 0, tiled=True)


def shards(velocity, below, above, omega_x, omega_y, omega_z, phi_x, phi_y, phi_z):
    total_x = 2048
    total_y = 1536
    total_z = 32
    gz = lax.axis_index("gz")
    near, x_high, x_low, y_high, y_low = pack(velocity)
    far = shift_permute(near, "gz", 1)
    sides = [
        shift_permute(x_high, "gx", 1),
        shift_permute(x_low, "gx", -1),
        shift_permute(y_high, "gy", 1),
        shift_permute(y_low, "gy", -1),
    ]
    send, mine, theirs = field(velocity, far, below, above, sides, omega_x, omega_y, omega_z, phi_x, phi_z)
    got = exchange(send, ("gx", "gz")).reshape(16, 2, 52, 128)
    part_x = mine + shift_permute(theirs, "gz", 1)

    by_z = jnp.sum(got, axis=0)
    summed = by_z[0] + by_z[1]
    same = jnp.where(gz == 0, by_z[0, 24:40], by_z[1, 24:40])
    cross = jnp.where(gz == 0, by_z[1, 24:40], by_z[0, 24:40])
    rows_z = jnp.concatenate(
        [same.reshape(2, 8, 128).transpose(1, 0, 2), cross.reshape(2, 8, 128).transpose(1, 0, 2)], axis=0
    )
    rest = jnp.concatenate([summed[16:24, :64], summed[16:24, 64:]], axis=0)
    lead_high, lead_low = split(jnp.concatenate([summed[:16], rest], axis=1))
    wide = phi_y.T.astype(jnp.bfloat16)
    none = jnp.zeros((96, 512), jnp.bfloat16)
    wide = jnp.concatenate(
        [jnp.concatenate([wide, none], axis=1), jnp.concatenate([none, wide], axis=1)], axis=0
    )
    core = jnp.dot(jnp.concatenate([lead_high, lead_low], axis=0), wide, preferred_element_type=jnp.float32)
    core = (core[:16] + core[16:]).reshape(16, 8, 128)
    send = jnp.concatenate([core, part_x.reshape(16, 8, 128), rows_z], axis=1)
    got = jnp.sum(exchange(send.reshape(288, 128), "gy").reshape(16, 18, 128), axis=0)
    core_sketch = got[:8].reshape(1, 2, 512) * (1.0 / math.sqrt(total_x * total_y * total_z))

    got_y = lax.all_gather(summed[40:52], "gx", axis=0, tiled=True).reshape(16, 2, 6, 128)
    factor_y = got_y.transpose(0, 2, 1, 3).reshape(96, 256)
    factor_y = factor_y * (1.0 / math.sqrt(total_x * total_z))

    got_x = exchange(jnp.broadcast_to(got[None, 8:18], (32, 10, 128)).reshape(320, 128), ("gy", "gz"))
    got_x = got_x.reshape(16, 2, 10, 128)
    factor_x = got_x[:, :, :8].transpose(0, 2, 1, 3).reshape(128, 256)
    factor_x = factor_x * (1.0 / math.sqrt(total_y * total_z))
    first, second = got_x[:, 0, 8:], got_x[:, 1, 8:]
    same = jnp.where(gz == 0, first[:8], second[:8])
    cross = jnp.where(gz == 0, second[8:], first[8:])
    factor_z = jnp.concatenate([same, cross], axis=0).reshape(16, 256) * (1.0 / math.sqrt(total_x * total_y))
    return (factor_x, factor_y, factor_z, core_sketch)


def solution(mesh):
    in_specs = (
        P(None, "gz", "gy", "gx"),
        P(None, None, "gy", "gx"),
        P(None, None, "gy", "gx"),
        P("gx", None),
        P("gy", None),
        P("gz", None),
        P(None, "gx"),
        P(None, "gy"),
        P(None, "gz"),
    )
    out_specs = (P("gx", None), P("gy", None), P("gz", None), P(("gx", "gy", "gz"), None, None))
    return jax.shard_map(shards, mesh=mesh, in_specs=in_specs, out_specs=out_specs, check_vma=False)
```

```python
import math

import jax
import jax.numpy as jnp
from jax import lax
from jax.experimental import pallas as pl
from jax.experimental.pallas import tpu as pltpu
from jax.sharding import PartitionSpec as P


def shift_permute(cells, axis, step):
    count = lax.axis_size(axis)
    return lax.ppermute(cells, axis, [(i, (i + step) % count) for i in range(count)])


def edge_swap(cells, axis, odd):
    count = lax.axis_size(axis)
    pairs = []
    for i in range(odd, count + odd, 2):
        pairs += [(i % count, (i + 1) % count), ((i + 1) % count, i % count)]
    return lax.ppermute(cells, axis, pairs)


def pack_kernel(vel, near, x_even, x_odd, y_even, y_odd, held, sems):
    gz = lax.axis_index("gz")
    odd_x = lax.rem(lax.axis_index("gx"), 2) == 1
    odd_y = lax.rem(lax.axis_index("gy"), 2) == 1
    copies = [
        pltpu.make_async_copy(
            vel.at[part // 2, pl.ds(8 * (part % 2), 8)], held.at[part // 2, pl.ds(8 * (part % 2), 8)], sems.at[part]
        )
        for part in range(6)
    ]
    for copy in copies:
        copy.start()
    lane = lax.broadcasted_iota(jnp.int32, (96, 128), 1)
    high = jnp.zeros((96, 128), jnp.float32)
    low = jnp.zeros((96, 128), jnp.float32)
    rims = []
    for part in range(6):
        copies[part].wait()
        c = part // 2
        if part % 2 == 1:
            rims.append(
                pltpu.make_async_copy(held.at[c, pl.ds(14 * (1 - gz), 2)], near.at[c], sems.at[6 + c])
            )
            rims[-1].start()
        for k in range(8 * (part % 2), 8 * (part % 2) + 8):
            spot = 2 * (16 * c + k)
            turned = pltpu.roll(held[c, k], spot + 2, 1)
            high = jnp.where((lane >= spot) & (lane < spot + 2), turned, high)
            low = jnp.where((lane >= spot + 2) & (lane < spot + 4), turned, low)
            first = held[c, k, 0:2, :]
            last = held[c, k, 94:96, :]
            y_even[c, 2 * k : 2 * k + 2, :] = jnp.where(odd_y, first, last)
            y_odd[c, 2 * k : 2 * k + 2, :] = jnp.where(odd_y, last, first)
    x_even[...] = jnp.where(odd_x, low, high)
    x_odd[...] = jnp.where(odd_x, high, low)
    for rim in rims:
        rim.wait()


def pack(velocity):
    rims = jax.ShapeDtypeStruct((96, 128), jnp.float32)
    rows = jax.ShapeDtypeStruct((3, 32, 128), jnp.float32)
    whole = pl.BlockSpec(memory_space=pltpu.VMEM)
    outside = pl.BlockSpec(memory_space=pl.ANY)
    return pl.pallas_call(
        pack_kernel,
        in_specs=[outside],
        out_specs=[outside] + [whole] * 4,
        out_shape=[jax.ShapeDtypeStruct((3, 2, 96, 128), jnp.float32), rims, rims, rows, rows],
        scratch_shapes=[pltpu.VMEM((3, 16, 96, 128), jnp.float32), pltpu.SemaphoreType.DMA((9,))],
        compiler_params=pltpu.CompilerParams(vmem_limit_bytes=60 * 1024 * 1024),
        name="pack_halos",
    )(velocity)


def field_kernel(
    vel, far, below, above, x_even, x_odd, y_even, y_odd, omega_x, omega_y, omega_z, phi_x, phi_z,
    send, mine, theirs,
    padded, sides, x_held, y_held, wx_held, wy_held, wz_held, px_held,
    q_terms, flat, flat_terms, wx, wyz, phx, part_y, part_z, lead, pz_held, sems,
):
    gz = lax.axis_index("gz")
    odd_x = lax.rem(lax.axis_index("gx"), 2)
    odd_y = lax.rem(lax.axis_index("gy"), 2)
    middle = pl.ds(8, 96)
    x_copies = [
        pltpu.make_async_copy(x_even, x_held.at[1 - odd_x], sems.at[0]),
        pltpu.make_async_copy(x_odd, x_held.at[odd_x], sems.at[1]),
    ]
    y_copies = [
        pltpu.make_async_copy(y_even, y_held.at[1 - odd_y], sems.at[2]),
        pltpu.make_async_copy(y_odd, y_held.at[odd_y], sems.at[3]),
    ]
    cells_copies = [
        pltpu.make_async_copy(vel.at[c], padded.at[c, pl.ds(2, 16), middle, :], sems.at[4 + c]) for c in range(3)
    ]
    far_low = pltpu.make_async_copy(far, padded.at[:, pl.ds(0, 2), middle, :], sems.at[7])
    far_high = pltpu.make_async_copy(far, padded.at[:, pl.ds(18, 2), middle, :], sems.at[8])
    rim_low = pltpu.make_async_copy(below, padded.at[:, pl.ds(0, 2), middle, :], sems.at[7])
    rim_high = pltpu.make_async_copy(above, padded.at[:, pl.ds(18, 2), middle, :], sems.at[8])
    weight_copies = [
        pltpu.make_async_copy(omega_x, wx_held, sems.at[9]),
        pltpu.make_async_copy(omega_y, wy_held, sems.at[10]),
        pltpu.make_async_copy(omega_z, wz_held, sems.at[11]),
        pltpu.make_async_copy(phi_x, px_held, sems.at[12]),
    ]
    z_copy = pltpu.make_async_copy(phi_z, pz_held, sems.at[13])
    for copy in x_copies + cells_copies + y_copies + [z_copy]:
        copy.start()

    @pl.when(gz == 0)
    def _():
        rim_low.start()
        far_high.start()

    @pl.when(gz == 1)
    def _():
        far_low.start()
        rim_high.start()

    for copy in weight_copies:
        copy.start()
    for copy in x_copies:
        copy.wait()

    lane_all = lax.broadcasted_iota(jnp.int32, (96, 128), 1)

    def place(k, carry):
        for c in range(3):
            spot = 2 * (16 * c + k)
            both = jnp.where(lane_all < spot + 2, x_held[0], x_held[1])
            sides[c, k] = pltpu.roll(both, 126 - spot, 1)
        return carry

    lax.fori_loop(0, 16, place, 0, unroll=2)

    for copy in y_copies + cells_copies + [z_copy]:
        copy.wait()
    for c in range(3):
        for k in range(16):
            padded[c, k + 2, 6:8, :] = y_held[0, c, 2 * k : 2 * k + 2, :]
            padded[c, k + 2, 104:106, :] = y_held[1, c, 2 * k : 2 * k + 2, :]
    flat[...] = jnp.zeros((256, 128), jnp.float32)

    @pl.when(gz == 0)
    def _():
        rim_low.wait()
        far_high.wait()

    @pl.when(gz == 1)
    def _():
        far_low.wait()
        rim_high.wait()

    lane = lax.broadcasted_iota(jnp.int32, (16, 128), 1)

    def plane(k, carry):
        weight = [pz_held[c, k].astype(jnp.float32) for c in range(2)]
        for block in range(6):
            row = 16 * block
            at = row + 8
            along = [[], [], []]
            for c in range(3):
                cells = padded[c, k + 2, at : at + 16, :]
                rim = sides[c, k, row : row + 16, :]
                outer = pltpu.roll(jnp.where(lane >= 126, rim, cells), 2, 1) - pltpu.roll(
                    jnp.where(lane < 2, rim, cells), 126, 1
                )
                inner = pltpu.roll(jnp.where(lane < 1, rim, cells), 127, 1) - pltpu.roll(
                    jnp.where(lane >= 127, rim, cells), 1, 1
                )
                along[0].append(outer + 8.0 * inner)
                outer = padded[c, k + 2, at - 2 : at + 14, :] - padded[c, k + 2, at + 2 : at + 18, :]
                inner = padded[c, k + 2, at + 1 : at + 17, :] - padded[c, k + 2, at - 1 : at + 15, :]
                along[1].append(outer + 8.0 * inner)
                outer = padded[c, k, at : at + 16, :] - padded[c, k + 4, at : at + 16, :]
                inner = padded[c, k + 3, at : at + 16, :] - padded[c, k + 1, at : at + 16, :]
                along[2].append(outer + 8.0 * inner)
            diagonal = along[0][0] * along[0][0] + along[1][1] * along[1][1] + along[2][2] * along[2][2]
            mixed = along[0][1] * along[1][0] + along[0][2] * along[2][0] + along[1][2] * along[2][1]
            field = (-0.5 / 144.0) * (diagonal + 2.0 * mixed)
            high = field.astype(jnp.bfloat16)
            low = (field - high.astype(jnp.float32)).astype(jnp.bfloat16)
            rows = pl.ds(pl.multiple_of(96 * k + row, 16), 16)
            q_terms[rows, 0:128] = high
            q_terms[rows, 128:256] = low
            for c in range(2):
                flat[96 * c + row : 96 * c + row + 16, :] += weight[c] * field
        return carry

    lax.fori_loop(0, 16, plane, 0, unroll=4)

    for copy in weight_copies:
        copy.wait()
    wx[0:128, :] = wx_held[...].astype(jnp.float32).astype(jnp.bfloat16)
    wx[128:256, :] = wx_held[...].astype(jnp.float32).astype(jnp.bfloat16)
    phx[:, 0:128] = px_held[...].astype(jnp.float32).astype(jnp.bfloat16)
    phx[:, 128:256] = px_held[...].astype(jnp.float32).astype(jnp.bfloat16)
    wy = wy_held[...].astype(jnp.float32)
    wz = wz_held[...].astype(jnp.float32)

    flat_high = flat[...].astype(jnp.bfloat16)
    flat_terms[:, 0:128] = flat_high
    flat_terms[:, 128:256] = (flat[...] - flat_high.astype(jnp.float32)).astype(jnp.bfloat16)
    leading = lax.dot_general(
        phx[...], flat_terms[...], (((1,), (1,)), ((), ())), preferred_element_type=jnp.float32
    )
    lead[0] = leading[:, 0:128]
    lead[1] = leading[:, 128:256]

    total_y = jnp.zeros((96, 256), jnp.float32)
    for k in range(16):
        rows = slice(96 * k, 96 * k + 96)
        sums = jnp.dot(q_terms[rows, :], wx[...], preferred_element_type=jnp.float32)
        total_y = total_y + sums * wz[k : k + 1, :]
        part_z[k : k + 1, :] = jnp.sum(sums * wy, axis=0, keepdims=True)
        wyz[rows, :] = (wy * wz[k : k + 1, :]).astype(jnp.bfloat16)
    part_y[...] = total_y

    lane8 = lax.broadcasted_iota(jnp.int32, (8, 128), 1)
    shares = [part_z[pl.ds(pl.multiple_of(8 * jnp.abs(z - gz), 8), 8), :] for z in range(2)]
    for g in range(16):
        for z in range(2):
            chunk = 2 * g + z
            base = 48 * chunk
            near = 32 * g + z
            send[base : base + 16, :] = lead[0, pl.ds(near, 16, stride=2), :]
            send[base + 16 : base + 24, :] = jnp.where(
                lane8 < 64,
                lead[1, pl.ds(near, 8, stride=2), :],
                pltpu.roll(lead[1, pl.ds(near + 16, 8, stride=2), :], 64, 1),
            )
            for half in range(2):
                lanes = slice(128 * half, 128 * half + 128)
                send[base + 24 + 8 * half : base + 32 + 8 * half, :] = shares[z][:, lanes]
                send[base + 40 + 3 * half : base + 43 + 3 * half, :] = part_y[3 * chunk : 3 * chunk + 3, lanes]
            send[base + 46 : base + 48, :] = jnp.zeros((2, 128), jnp.float32)

    turned = lax.dot_general(
        q_terms[...], wyz[...], (((0,), (0,)), ((), ())), preferred_element_type=jnp.float32
    )
    turned = turned[0:128, :] + turned[128:256, :]
    mine[...] = jnp.where(gz == 0, turned[:, 0:128], turned[:, 128:256])
    theirs[...] = jnp.where(gz == 0, turned[:, 128:256], turned[:, 0:128])


def field(velocity, far, below, above, sides, omega_x, omega_y, omega_z, phi_x, phi_z):
    whole = pl.BlockSpec(memory_space=pltpu.VMEM)
    outside = pl.BlockSpec(memory_space=pl.ANY)
    half = jax.ShapeDtypeStruct((128, 128), jnp.float32)
    return pl.pallas_call(
        field_kernel,
        in_specs=[outside] * 13,
        out_specs=[whole] * 3,
        out_shape=[jax.ShapeDtypeStruct((1536, 128), jnp.float32), half, half],
        scratch_shapes=[
            pltpu.VMEM((3, 20, 112, 128), jnp.float32),
            pltpu.VMEM((3, 16, 96, 128), jnp.float32),
            pltpu.VMEM((2, 96, 128), jnp.float32),
            pltpu.VMEM((2, 3, 32, 128), jnp.float32),
            pltpu.VMEM((128, 256), jnp.int32),
            pltpu.VMEM((96, 256), jnp.int32),
            pltpu.VMEM((16, 256), jnp.int32),
            pltpu.VMEM((512, 128), jnp.int32),
            pltpu.VMEM((1536, 256), jnp.bfloat16),
            pltpu.VMEM((256, 128), jnp.float32),
            pltpu.VMEM((256, 256), jnp.bfloat16),
            pltpu.VMEM((256, 256), jnp.bfloat16),
            pltpu.VMEM((1536, 256), jnp.bfloat16),
            pltpu.VMEM((512, 256), jnp.bfloat16),
            pltpu.VMEM((96, 256), jnp.float32),
            pltpu.VMEM((16, 256), jnp.float32),
            pltpu.VMEM((2, 512, 128), jnp.float32),
            pltpu.SMEM((2, 16), jnp.int32),
            pltpu.SemaphoreType.DMA((14,)),
        ],
        compiler_params=pltpu.CompilerParams(vmem_limit_bytes=60 * 1024 * 1024),
        name="field_products",
    )(velocity, far, below, above, *sides, omega_x, omega_y, omega_z, phi_x, phi_z)


def split(values):
    high = lax.reduce_precision(values, 8, 7)
    return high.astype(jnp.bfloat16), (values - high).astype(jnp.bfloat16)


def exchange(rows, axes):
    return lax.all_to_all(rows, axes, 0, 0, tiled=True)


def shards(velocity, below, above, omega_x, omega_y, omega_z, phi_x, phi_y, phi_z):
    total_x = 2048
    total_y = 1536
    total_z = 32
    gz = lax.axis_index("gz")
    near, x_even, x_odd, y_even, y_odd = pack(velocity)
    far = shift_permute(near, "gz", 1)
    sides = [
        edge_swap(x_even, "gx", 0),
        edge_swap(x_odd, "gx", 1),
        edge_swap(y_even, "gy", 0),
        edge_swap(y_odd, "gy", 1),
    ]
    send, mine, theirs = field(velocity, far, below, above, sides, omega_x, omega_y, omega_z, phi_x, phi_z)
    got = exchange(send, ("gx", "gz")).reshape(16, 2, 48, 128)
    part_x = mine + shift_permute(theirs, "gz", 1)

    by_z = jnp.sum(got, axis=0)
    summed = by_z[0] + by_z[1]
    same = jnp.where(gz == 0, by_z[0, 24:40], by_z[1, 24:40])
    cross = jnp.where(gz == 0, by_z[1, 24:40], by_z[0, 24:40])
    rows_z = jnp.concatenate(
        [same.reshape(2, 8, 128).transpose(1, 0, 2), cross.reshape(2, 8, 128).transpose(1, 0, 2)], axis=0
    )
    rest = jnp.concatenate([summed[16:24, :64], summed[16:24, 64:]], axis=0)
    lead_high, lead_low = split(jnp.concatenate([summed[:16], rest], axis=1))
    wide = phi_y.T.astype(jnp.bfloat16)
    none = jnp.zeros((96, 512), jnp.bfloat16)
    wide = jnp.concatenate(
        [jnp.concatenate([wide, none], axis=1), jnp.concatenate([none, wide], axis=1)], axis=0
    )
    core = jnp.dot(jnp.concatenate([lead_high, lead_low], axis=0), wide, preferred_element_type=jnp.float32)
    core = (core[:16] + core[16:]).reshape(16, 8, 128)
    send = jnp.concatenate([core, part_x.reshape(16, 8, 128), rows_z], axis=1)
    got = jnp.sum(exchange(send.reshape(16, 9, 2, 128), "gy"), axis=0).reshape(18, 128)
    core_sketch = got[:8].reshape(1, 2, 512) * (1.0 / math.sqrt(total_x * total_y * total_z))

    got_y = lax.all_gather(summed[40:46], "gx", axis=0, tiled=True)
    rows, got_y = lax.optimization_barrier((got[8:18], got_y))
    other_y = shift_permute(got_y, "gz", 1)
    halves = [jnp.where(gz == z, got_y, other_y).reshape(16, 2, 3, 128).transpose(0, 2, 1, 3) for z in range(2)]
    factor_y = jnp.stack(halves, axis=1).reshape(96, 256) * (1.0 / math.sqrt(total_x * total_z))

    got_x = exchange(jnp.broadcast_to(rows.reshape(1, 5, 2, 128), (32, 5, 2, 128)), ("gy", "gz"))
    got_x = got_x.reshape(16, 2, 10, 128)
    factor_x = got_x[:, :, :8].transpose(0, 2, 1, 3).reshape(128, 256)
    factor_x = factor_x * (1.0 / math.sqrt(total_y * total_z))
    first, second = got_x[:, 0, 8:], got_x[:, 1, 8:]
    same = jnp.where(gz == 0, first[:8], second[:8])
    cross = jnp.where(gz == 0, second[8:], first[8:])
    factor_z = jnp.concatenate([same, cross], axis=0).reshape(16, 256) * (1.0 / math.sqrt(total_x * total_y))
    return (factor_x, factor_y, factor_z, core_sketch)


def solution(mesh):
    in_specs = (
        P(None, "gz", "gy", "gx"),
        P(None, None, "gy", "gx"),
        P(None, None, "gy", "gx"),
        P("gx", None),
        P("gy", None),
        P("gz", None),
        P(None, "gx"),
        P(None, "gy"),
        P(None, "gz"),
    )
    out_specs = (P("gx", None), P("gy", None), P("gz", None), P(("gx", "gy", "gz"), None, None))
    return jax.shard_map(shards, mesh=mesh, in_specs=in_specs, out_specs=out_specs, check_vma=False)
```

```python
import math

import jax
import jax.numpy as jnp
from jax import lax
from jax.experimental import pallas as pl
from jax.experimental.pallas import tpu as pltpu
from jax.sharding import PartitionSpec as P


def shift_permute(cells, axis, step):
    count = lax.axis_size(axis)
    return lax.ppermute(cells, axis, [(i, (i + step) % count) for i in range(count)])


def edge_swap(cells, axis, odd):
    count = lax.axis_size(axis)
    pairs = []
    for i in range(odd, count + odd, 2):
        pairs += [(i % count, (i + 1) % count), ((i + 1) % count, i % count)]
    return lax.ppermute(cells, axis, pairs)


def pack_kernel(vel, near, x_even, x_odd, y_even, y_odd):
    gz = lax.axis_index("gz")
    odd_x = lax.rem(lax.axis_index("gx"), 2) == 1
    odd_y = lax.rem(lax.axis_index("gy"), 2) == 1
    lane = lax.broadcasted_iota(jnp.int32, (96, 128), 1)
    high = jnp.zeros((96, 128), jnp.float32)
    low = jnp.zeros((96, 128), jnp.float32)
    for c in range(3):
        near[c] = vel[c, pl.ds(14 * (1 - gz), 2)]
        for k in range(16):
            spot = 2 * (16 * c + k)
            turned = pltpu.roll(vel[c, k], spot + 2, 1)
            high = jnp.where((lane >= spot) & (lane < spot + 2), turned, high)
            low = jnp.where((lane >= spot + 2) & (lane < spot + 4), turned, low)
            first = vel[c, k, 0:2, :]
            last = vel[c, k, 94:96, :]
            y_even[c, 2 * k : 2 * k + 2, :] = jnp.where(odd_y, first, last)
            y_odd[c, 2 * k : 2 * k + 2, :] = jnp.where(odd_y, last, first)
    x_even[...] = jnp.where(odd_x, low, high)
    x_odd[...] = jnp.where(odd_x, high, low)


def pack(velocity):
    rims = jax.ShapeDtypeStruct((96, 128), jnp.float32)
    rows = jax.ShapeDtypeStruct((3, 32, 128), jnp.float32)
    whole = pl.BlockSpec(memory_space=pltpu.VMEM)
    return pl.pallas_call(
        pack_kernel,
        in_specs=[whole],
        out_specs=[whole] * 5,
        out_shape=[jax.ShapeDtypeStruct((3, 2, 96, 128), jnp.float32), rims, rims, rows, rows],
        compiler_params=pltpu.CompilerParams(vmem_limit_bytes=32 * 1024 * 1024),
        name="pack_halos",
    )(velocity)


def field_kernel(
    vel, far, below, above, y_even, y_odd, x_odd, x_even, omega_x, omega_y, omega_z, phi_x, phi_z,
    send, mine, theirs,
    padded, sides, x_held, y_held, wx_held, wy_held, wz_held, px_held,
    q_terms, flat, flat_terms, wx, wyz, phx, part_y, part_z, lead, pz_held, sems,
):
    gz = lax.axis_index("gz")
    odd_x = lax.rem(lax.axis_index("gx"), 2)
    odd_y = lax.rem(lax.axis_index("gy"), 2)
    middle = pl.ds(8, 96)
    x_copies = [
        pltpu.make_async_copy(x_even, x_held.at[1 - odd_x], sems.at[0]),
        pltpu.make_async_copy(x_odd, x_held.at[odd_x], sems.at[1]),
    ]
    y_copies = [
        pltpu.make_async_copy(y_even, y_held.at[1 - odd_y], sems.at[2]),
        pltpu.make_async_copy(y_odd, y_held.at[odd_y], sems.at[3]),
    ]
    cells_copies = [
        pltpu.make_async_copy(vel.at[c], padded.at[c, pl.ds(2, 16), middle, :], sems.at[4 + c]) for c in range(3)
    ]
    far_low = pltpu.make_async_copy(far, padded.at[:, pl.ds(0, 2), middle, :], sems.at[7])
    far_high = pltpu.make_async_copy(far, padded.at[:, pl.ds(18, 2), middle, :], sems.at[8])
    rim_low = pltpu.make_async_copy(below, padded.at[:, pl.ds(0, 2), middle, :], sems.at[7])
    rim_high = pltpu.make_async_copy(above, padded.at[:, pl.ds(18, 2), middle, :], sems.at[8])
    weight_copies = [
        pltpu.make_async_copy(omega_x, wx_held, sems.at[9]),
        pltpu.make_async_copy(omega_y, wy_held, sems.at[10]),
        pltpu.make_async_copy(omega_z, wz_held, sems.at[11]),
        pltpu.make_async_copy(phi_x, px_held, sems.at[12]),
    ]
    z_copy = pltpu.make_async_copy(phi_z, pz_held, sems.at[13])
    for copy in x_copies + cells_copies + y_copies + [z_copy]:
        copy.start()

    @pl.when(gz == 0)
    def _():
        rim_low.start()
        far_high.start()

    @pl.when(gz == 1)
    def _():
        far_low.start()
        rim_high.start()

    for copy in weight_copies:
        copy.start()
    for copy in x_copies:
        copy.wait()

    lane_all = lax.broadcasted_iota(jnp.int32, (96, 128), 1)

    def place(k, carry):
        for c in range(3):
            spot = 2 * (16 * c + k)
            both = jnp.where(lane_all < spot + 2, x_held[0], x_held[1])
            sides[c, k] = pltpu.roll(both, 126 - spot, 1)
        return carry

    lax.fori_loop(0, 16, place, 0, unroll=2)

    for copy in y_copies + cells_copies + [z_copy]:
        copy.wait()
    for c in range(3):
        for k in range(16):
            padded[c, k + 2, 6:8, :] = y_held[0, c, 2 * k : 2 * k + 2, :]
            padded[c, k + 2, 104:106, :] = y_held[1, c, 2 * k : 2 * k + 2, :]
    flat[...] = jnp.zeros((256, 128), jnp.float32)

    @pl.when(gz == 0)
    def _():
        rim_low.wait()
        far_high.wait()

    @pl.when(gz == 1)
    def _():
        far_low.wait()
        rim_high.wait()

    lane = lax.broadcasted_iota(jnp.int32, (16, 128), 1)

    def plane(k, carry):
        weight = [pz_held[c, k].astype(jnp.float32) for c in range(2)]
        for block in range(6):
            row = 16 * block
            at = row + 8
            along = [[], [], []]
            for c in range(3):
                cells = padded[c, k + 2, at : at + 16, :]
                rim = sides[c, k, row : row + 16, :]
                outer = pltpu.roll(jnp.where(lane >= 126, rim, cells), 2, 1) - pltpu.roll(
                    jnp.where(lane < 2, rim, cells), 126, 1
                )
                inner = pltpu.roll(jnp.where(lane < 1, rim, cells), 127, 1) - pltpu.roll(
                    jnp.where(lane >= 127, rim, cells), 1, 1
                )
                along[0].append(outer + 8.0 * inner)
                outer = padded[c, k + 2, at - 2 : at + 14, :] - padded[c, k + 2, at + 2 : at + 18, :]
                inner = padded[c, k + 2, at + 1 : at + 17, :] - padded[c, k + 2, at - 1 : at + 15, :]
                along[1].append(outer + 8.0 * inner)
                outer = padded[c, k, at : at + 16, :] - padded[c, k + 4, at : at + 16, :]
                inner = padded[c, k + 3, at : at + 16, :] - padded[c, k + 1, at : at + 16, :]
                along[2].append(outer + 8.0 * inner)
            diagonal = along[0][0] * along[0][0] + along[1][1] * along[1][1] + along[2][2] * along[2][2]
            mixed = along[0][1] * along[1][0] + along[0][2] * along[2][0] + along[1][2] * along[2][1]
            field = (-0.5 / 144.0) * (diagonal + 2.0 * mixed)
            high = field.astype(jnp.bfloat16)
            low = (field - high.astype(jnp.float32)).astype(jnp.bfloat16)
            rows = pl.ds(pl.multiple_of(96 * k + row, 16), 16)
            q_terms[rows, 0:128] = high
            q_terms[rows, 128:256] = low
            for c in range(2):
                flat[96 * c + row : 96 * c + row + 16, :] += weight[c] * field
        return carry

    lax.fori_loop(0, 16, plane, 0, unroll=4)

    for copy in weight_copies:
        copy.wait()
    wx[0:128, :] = wx_held[...].astype(jnp.float32).astype(jnp.bfloat16)
    wx[128:256, :] = wx_held[...].astype(jnp.float32).astype(jnp.bfloat16)
    phx[:, 0:128] = px_held[...].astype(jnp.float32).astype(jnp.bfloat16)
    phx[:, 128:256] = px_held[...].astype(jnp.float32).astype(jnp.bfloat16)
    wy = wy_held[...].astype(jnp.float32)
    wz = wz_held[...].astype(jnp.float32)

    flat_high = flat[...].astype(jnp.bfloat16)
    flat_terms[:, 0:128] = flat_high
    flat_terms[:, 128:256] = (flat[...] - flat_high.astype(jnp.float32)).astype(jnp.bfloat16)
    leading = lax.dot_general(
        phx[...], flat_terms[...], (((1,), (1,)), ((), ())), preferred_element_type=jnp.float32
    )
    lead[0] = leading[:, 0:128]
    lead[1] = leading[:, 128:256]

    total_y = jnp.zeros((96, 256), jnp.float32)
    for k in range(16):
        rows = slice(96 * k, 96 * k + 96)
        sums = jnp.dot(q_terms[rows, :], wx[...], preferred_element_type=jnp.float32)
        total_y = total_y + sums * wz[k : k + 1, :]
        part_z[k : k + 1, :] = jnp.sum(sums * wy, axis=0, keepdims=True)
        wyz[rows, :] = (wy * wz[k : k + 1, :]).astype(jnp.bfloat16)
    part_y[...] = total_y

    lane8 = lax.broadcasted_iota(jnp.int32, (8, 128), 1)
    for g in range(16):
        for z in range(2):
            chunk = 2 * g + z
            base = 32 * chunk
            near = 32 * g + z
            send[base : base + 16, :] = lead[0, pl.ds(near, 16, stride=2), :]
            send[base + 16 : base + 24, :] = jnp.where(
                lane8 < 64,
                lead[1, pl.ds(near, 8, stride=2), :],
                pltpu.roll(lead[1, pl.ds(near + 16, 8, stride=2), :], 64, 1),
            )
            for half in range(2):
                lanes = slice(128 * half, 128 * half + 128)
                send[base + 24 + 3 * half : base + 27 + 3 * half, :] = part_y[3 * chunk : 3 * chunk + 3, lanes]
                send[base + 30 + half : base + 31 + half, :] = part_z[g : g + 1, lanes]

    turned = lax.dot_general(
        q_terms[...], wyz[...], (((0,), (0,)), ((), ())), preferred_element_type=jnp.float32
    )
    turned = turned[0:128, :] + turned[128:256, :]
    mine[...] = jnp.where(gz == 0, turned[:, 0:128], turned[:, 128:256])
    theirs[...] = jnp.where(gz == 0, turned[:, 128:256], turned[:, 0:128])


def field(velocity, far, below, above, sides, omega_x, omega_y, omega_z, phi_x, phi_z):
    whole = pl.BlockSpec(memory_space=pltpu.VMEM)
    outside = pl.BlockSpec(memory_space=pl.ANY)
    half = jax.ShapeDtypeStruct((128, 128), jnp.float32)
    return pl.pallas_call(
        field_kernel,
        in_specs=[outside] * 13,
        out_specs=[whole] * 3,
        out_shape=[jax.ShapeDtypeStruct((1024, 128), jnp.float32), half, half],
        scratch_shapes=[
            pltpu.VMEM((3, 20, 112, 128), jnp.float32),
            pltpu.VMEM((3, 16, 96, 128), jnp.float32),
            pltpu.VMEM((2, 96, 128), jnp.float32),
            pltpu.VMEM((2, 3, 32, 128), jnp.float32),
            pltpu.VMEM((128, 256), jnp.int32),
            pltpu.VMEM((96, 256), jnp.int32),
            pltpu.VMEM((16, 256), jnp.int32),
            pltpu.VMEM((512, 128), jnp.int32),
            pltpu.VMEM((1536, 256), jnp.bfloat16),
            pltpu.VMEM((256, 128), jnp.float32),
            pltpu.VMEM((256, 256), jnp.bfloat16),
            pltpu.VMEM((256, 256), jnp.bfloat16),
            pltpu.VMEM((1536, 256), jnp.bfloat16),
            pltpu.VMEM((512, 256), jnp.bfloat16),
            pltpu.VMEM((96, 256), jnp.float32),
            pltpu.VMEM((16, 256), jnp.float32),
            pltpu.VMEM((2, 512, 128), jnp.float32),
            pltpu.SMEM((2, 16), jnp.int32),
            pltpu.SemaphoreType.DMA((14,)),
        ],
        compiler_params=pltpu.CompilerParams(vmem_limit_bytes=32 * 1024 * 1024),
        name="field_products",
    )(velocity, far, below, above, *sides, omega_x, omega_y, omega_z, phi_x, phi_z)


def split(values):
    high = lax.reduce_precision(values, 8, 7)
    return high.astype(jnp.bfloat16), (values - high).astype(jnp.bfloat16)


FAR = [[4 * x + r for x in range(4)] for r in range(4)]
NEAR = [[4 * x + r for r in range(4)] for x in range(4)]
FAR_Z = [[8 * x + r for x in range(4)] for r in range(8)]
NEAR_Z = [[8 * x + r for r in range(8)] for x in range(4)]


def gather(rows, axes, groups):
    return lax.all_gather(rows, axes, axis=0, tiled=True, axis_index_groups=groups)


def unfold_kernel(wide_y, wide_z, factor_y, factor_z):
    scale_y = 1.0 / math.sqrt(2048 * 32)
    scale_z = 1.0 / math.sqrt(2048 * 1536)
    for g in range(16):
        x, near = g // 4, g % 4
        for half in range(2):
            lanes = slice(128 * half, 128 * half + 128)
            for z in range(2):
                spot = 24 * (2 * near + z) + 6 * x + 3 * half
                factor_y[6 * g + 3 * z : 6 * g + 3 * z + 3, lanes] = wide_y[spot : spot + 3, :] * scale_y
            spot = 8 * near + 2 * x + half
            factor_z[g : g + 1, lanes] = wide_z[spot : spot + 1, :] * scale_z


def unfold(wide_y, wide_z):
    whole = pl.BlockSpec(memory_space=pltpu.VMEM)
    return pl.pallas_call(
        unfold_kernel,
        in_specs=[whole] * 2,
        out_specs=[whole] * 2,
        out_shape=[jax.ShapeDtypeStruct((96, 256), jnp.float32), jax.ShapeDtypeStruct((16, 256), jnp.float32)],
        compiler_params=pltpu.CompilerParams(vmem_limit_bytes=4 * 1024 * 1024),
        cost_estimate=pl.CostEstimate(flops=0, bytes_accessed=0, transcendentals=0),
        name="unfold_factors",
    )(wide_y, wide_z)


def exchange(rows, axes):
    return lax.all_to_all(rows, axes, 0, 0, tiled=True)


def shards(velocity, below, above, omega_x, omega_y, omega_z, phi_x, phi_y, phi_z):
    total_x = 2048
    total_y = 1536
    total_z = 32
    gz = lax.axis_index("gz")
    near, x_even, x_odd, y_even, y_odd = pack(velocity)
    far = shift_permute(near, "gz", 1)
    y_even = edge_swap(y_even, "gy", 0)
    y_odd = edge_swap(y_odd, "gy", 1)
    x_odd = edge_swap(x_odd, "gx", 1)
    x_even = edge_swap(x_even, "gx", 0)
    sides = [y_even, y_odd, x_odd, x_even]
    send, mine, theirs = field(velocity, far, below, above, sides, omega_x, omega_y, omega_z, phi_x, phi_z)
    got = exchange(send, ("gx", "gz")).reshape(16, 2, 32, 128)
    part_x = mine + shift_permute(theirs, "gz", 1)

    by_z = jnp.sum(got, axis=0)
    summed = by_z[0] + by_z[1]
    summed_z = jnp.where(gz == 0, by_z[0, 30:32], by_z[1, 30:32])
    rest = jnp.concatenate([summed[16:24, :64], summed[16:24, 64:]], axis=0)
    lead_high, lead_low = split(jnp.concatenate([summed[:16], rest], axis=1))
    wide = phi_y.T.astype(jnp.bfloat16)
    none = jnp.zeros((96, 512), jnp.bfloat16)
    wide = jnp.concatenate(
        [jnp.concatenate([wide, none], axis=1), jnp.concatenate([none, wide], axis=1)], axis=0
    )
    core = jnp.dot(jnp.concatenate([lead_high, lead_low], axis=0), wide, preferred_element_type=jnp.float32)
    core = (core[:16] + core[16:]).reshape(16, 8, 128)
    rows_z = jnp.broadcast_to(summed_z[None], (16, 2, 128))
    send = jnp.concatenate([core, part_x.reshape(16, 8, 128), rows_z], axis=1)
    got = jnp.sum(exchange(send.reshape(288, 128), "gy").reshape(16, 18, 128), axis=0)
    core_sketch = got[:8].reshape(1, 2, 512) * (1.0 / math.sqrt(total_x * total_y * total_z))

    part_y = gather(gather(summed[24:30], ("gx", "gz"), FAR_Z), ("gx", "gz"), NEAR_Z)
    rows, part_y = lax.optimization_barrier((got[8:18], part_y))
    got_x = exchange(jnp.broadcast_to(rows[None, :8], (32, 8, 128)).reshape(256, 128), ("gy", "gz"))
    part_z = gather(gather(rows[8:], "gx", FAR), "gx", NEAR)
    factor_y, factor_z = unfold(part_y, part_z)

    factor_x = got_x.reshape(16, 2, 8, 128).transpose(0, 2, 1, 3).reshape(128, 256)
    factor_x = factor_x * (1.0 / math.sqrt(total_y * total_z))
    return (factor_x, factor_y, factor_z, core_sketch)


def solution(mesh):
    in_specs = (
        P(None, "gz", "gy", "gx"),
        P(None, None, "gy", "gx"),
        P(None, None, "gy", "gx"),
        P("gx", None),
        P("gy", None),
        P("gz", None),
        P(None, "gx"),
        P(None, "gy"),
        P(None, "gz"),
    )
    out_specs = (P("gx", None), P("gy", None), P("gz", None), P(("gx", "gy", "gz"), None, None))
    return jax.shard_map(shards, mesh=mesh, in_specs=in_specs, out_specs=out_specs, check_vma=False)
```

```python
import math

import jax
import jax.numpy as jnp
from jax import lax
from jax.experimental import pallas as pl
from jax.experimental.pallas import tpu as pltpu
from jax.sharding import PartitionSpec as P


def shift_permute(cells, axis, step):
    count = lax.axis_size(axis)
    return lax.ppermute(cells, axis, [(i, (i + step) % count) for i in range(count)])


def edge_swap(cells, axis, odd):
    count = lax.axis_size(axis)
    pairs = []
    for i in range(odd, count + odd, 2):
        pairs += [(i % count, (i + 1) % count), ((i + 1) % count, i % count)]
    return lax.ppermute(cells, axis, pairs)


def pack_kernel(vel, near, x_even, x_odd, y_even, y_odd):
    gz = lax.axis_index("gz")
    odd_x = lax.rem(lax.axis_index("gx"), 2) == 1
    odd_y = lax.rem(lax.axis_index("gy"), 2) == 1
    lane = lax.broadcasted_iota(jnp.int32, (96, 128), 1)
    high = jnp.zeros((96, 128), jnp.float32)
    low = jnp.zeros((96, 128), jnp.float32)
    for c in range(3):
        near[c] = vel[c, pl.ds(14 * (1 - gz), 2)]
        for k in range(16):
            spot = 2 * (16 * c + k)
            turned = pltpu.roll(vel[c, k], spot + 2, 1)
            high = jnp.where((lane >= spot) & (lane < spot + 2), turned, high)
            low = jnp.where((lane >= spot + 2) & (lane < spot + 4), turned, low)
            first = vel[c, k, 0:2, :]
            last = vel[c, k, 94:96, :]
            y_even[c, 2 * k : 2 * k + 2, :] = jnp.where(odd_y, first, last)
            y_odd[c, 2 * k : 2 * k + 2, :] = jnp.where(odd_y, last, first)
    x_even[...] = jnp.where(odd_x, low, high)
    x_odd[...] = jnp.where(odd_x, high, low)


def pack(velocity):
    rims = jax.ShapeDtypeStruct((96, 128), jnp.float32)
    rows = jax.ShapeDtypeStruct((3, 32, 128), jnp.float32)
    whole = pl.BlockSpec(memory_space=pltpu.VMEM)
    return pl.pallas_call(
        pack_kernel,
        in_specs=[whole],
        out_specs=[whole] * 5,
        out_shape=[jax.ShapeDtypeStruct((3, 2, 96, 128), jnp.float32), rims, rims, rows, rows],
        compiler_params=pltpu.CompilerParams(vmem_limit_bytes=32 * 1024 * 1024),
        name="pack_halos",
    )(velocity)


def field_kernel(
    vel, far, below, above, y_even, y_odd, x_odd, x_even, omega_x, omega_y, omega_z, phi_x, phi_z,
    send, mine, theirs,
    padded, sides, x_held, y_held, wx_held, wy_held, wz_held, px_held,
    q_terms, flat, flat_terms, wx, wyz, phx, part_y, part_z, lead, pz_held, sems,
):
    gz = lax.axis_index("gz")
    odd_x = lax.rem(lax.axis_index("gx"), 2)
    odd_y = lax.rem(lax.axis_index("gy"), 2)
    middle = pl.ds(8, 96)
    x_copies = [
        pltpu.make_async_copy(x_even, x_held.at[1 - odd_x], sems.at[0]),
        pltpu.make_async_copy(x_odd, x_held.at[odd_x], sems.at[1]),
    ]
    y_copies = [
        pltpu.make_async_copy(y_even, y_held.at[1 - odd_y], sems.at[2]),
        pltpu.make_async_copy(y_odd, y_held.at[odd_y], sems.at[3]),
    ]
    cells_copies = [
        pltpu.make_async_copy(vel.at[c], padded.at[c, pl.ds(2, 16), middle, :], sems.at[4 + c]) for c in range(3)
    ]
    far_low = pltpu.make_async_copy(far, padded.at[:, pl.ds(0, 2), middle, :], sems.at[7])
    far_high = pltpu.make_async_copy(far, padded.at[:, pl.ds(18, 2), middle, :], sems.at[8])
    rim_low = pltpu.make_async_copy(below, padded.at[:, pl.ds(0, 2), middle, :], sems.at[7])
    rim_high = pltpu.make_async_copy(above, padded.at[:, pl.ds(18, 2), middle, :], sems.at[8])
    weight_copies = [
        pltpu.make_async_copy(omega_x, wx_held, sems.at[9]),
        pltpu.make_async_copy(omega_y, wy_held, sems.at[10]),
        pltpu.make_async_copy(omega_z, wz_held, sems.at[11]),
        pltpu.make_async_copy(phi_x, px_held, sems.at[12]),
    ]
    z_copy = pltpu.make_async_copy(phi_z, pz_held, sems.at[13])
    for copy in x_copies + cells_copies + y_copies + [z_copy]:
        copy.start()

    @pl.when(gz == 0)
    def _():
        rim_low.start()
        far_high.start()

    @pl.when(gz == 1)
    def _():
        far_low.start()
        rim_high.start()

    for copy in weight_copies:
        copy.start()
    for copy in x_copies:
        copy.wait()

    lane_all = lax.broadcasted_iota(jnp.int32, (96, 128), 1)

    def place(k, carry):
        for c in range(3):
            spot = 2 * (16 * c + k)
            both = jnp.where(lane_all < spot + 2, x_held[0], x_held[1])
            sides[c, k] = pltpu.roll(both, 126 - spot, 1)
        return carry

    lax.fori_loop(0, 16, place, 0, unroll=2)

    for copy in y_copies + cells_copies + [z_copy]:
        copy.wait()
    for c in range(3):
        for k in range(16):
            padded[c, k + 2, 6:8, :] = y_held[0, c, 2 * k : 2 * k + 2, :]
            padded[c, k + 2, 104:106, :] = y_held[1, c, 2 * k : 2 * k + 2, :]
    flat[...] = jnp.zeros((256, 128), jnp.float32)

    @pl.when(gz == 0)
    def _():
        rim_low.wait()
        far_high.wait()

    @pl.when(gz == 1)
    def _():
        far_low.wait()
        rim_high.wait()

    lane = lax.broadcasted_iota(jnp.int32, (16, 128), 1)

    def plane(k, carry):
        weight = [pz_held[c, k].astype(jnp.float32) for c in range(2)]
        for block in range(6):
            row = 16 * block
            at = row + 8
            along = [[], [], []]
            for c in range(3):
                cells = padded[c, k + 2, at : at + 16, :]
                rim = sides[c, k, row : row + 16, :]
                outer = pltpu.roll(jnp.where(lane >= 126, rim, cells), 2, 1) - pltpu.roll(
                    jnp.where(lane < 2, rim, cells), 126, 1
                )
                inner = pltpu.roll(jnp.where(lane < 1, rim, cells), 127, 1) - pltpu.roll(
                    jnp.where(lane >= 127, rim, cells), 1, 1
                )
                along[0].append(outer + 8.0 * inner)
                outer = padded[c, k + 2, at - 2 : at + 14, :] - padded[c, k + 2, at + 2 : at + 18, :]
                inner = padded[c, k + 2, at + 1 : at + 17, :] - padded[c, k + 2, at - 1 : at + 15, :]
                along[1].append(outer + 8.0 * inner)
                outer = padded[c, k, at : at + 16, :] - padded[c, k + 4, at : at + 16, :]
                inner = padded[c, k + 3, at : at + 16, :] - padded[c, k + 1, at : at + 16, :]
                along[2].append(outer + 8.0 * inner)
            diagonal = along[0][0] * along[0][0] + along[1][1] * along[1][1] + along[2][2] * along[2][2]
            mixed = along[0][1] * along[1][0] + along[0][2] * along[2][0] + along[1][2] * along[2][1]
            field = (-0.5 / 144.0) * (diagonal + 2.0 * mixed)
            high = field.astype(jnp.bfloat16)
            low = (field - high.astype(jnp.float32)).astype(jnp.bfloat16)
            rows = pl.ds(pl.multiple_of(96 * k + row, 16), 16)
            q_terms[rows, 0:128] = high
            q_terms[rows, 128:256] = low
            for c in range(2):
                flat[96 * c + row : 96 * c + row + 16, :] += weight[c] * field
        return carry

    lax.fori_loop(0, 16, plane, 0, unroll=4)

    for copy in weight_copies:
        copy.wait()
    wx[0:128, :] = wx_held[...].astype(jnp.float32).astype(jnp.bfloat16)
    wx[128:256, :] = wx_held[...].astype(jnp.float32).astype(jnp.bfloat16)
    phx[:, 0:128] = px_held[...].astype(jnp.float32).astype(jnp.bfloat16)
    phx[:, 128:256] = px_held[...].astype(jnp.float32).astype(jnp.bfloat16)
    wy = wy_held[...].astype(jnp.float32)
    wz = wz_held[...].astype(jnp.float32)

    flat_high = flat[...].astype(jnp.bfloat16)
    flat_terms[:, 0:128] = flat_high
    flat_terms[:, 128:256] = (flat[...] - flat_high.astype(jnp.float32)).astype(jnp.bfloat16)
    leading = lax.dot_general(
        phx[...], flat_terms[...], (((1,), (1,)), ((), ())), preferred_element_type=jnp.float32
    )
    lead[0] = leading[:, 0:128]
    lead[1] = leading[:, 128:256]

    total_y = jnp.zeros((96, 256), jnp.float32)
    for k in range(16):
        rows = slice(96 * k, 96 * k + 96)
        sums = jnp.dot(q_terms[rows, :], wx[...], preferred_element_type=jnp.float32)
        total_y = total_y + sums * wz[k : k + 1, :]
        part_z[k : k + 1, :] = jnp.sum(sums * wy, axis=0, keepdims=True)
        wyz[rows, :] = (wy * wz[k : k + 1, :]).astype(jnp.bfloat16)
    part_y[...] = total_y

    lane8 = lax.broadcasted_iota(jnp.int32, (8, 128), 1)
    for g in range(16):
        for z in range(2):
            chunk = 2 * g + z
            base = 40 * chunk
            near = 32 * g + z
            send[base : base + 16, :] = lead[0, pl.ds(near, 16, stride=2), :]
            send[base + 16 : base + 24, :] = jnp.where(
                lane8 < 64,
                lead[1, pl.ds(near, 8, stride=2), :],
                pltpu.roll(lead[1, pl.ds(near + 16, 8, stride=2), :], 64, 1),
            )
            rank = 4 * ((g // 4) % 2) + g % 4
            spot = 6 * (2 * rank + z)
            for half in range(2):
                lanes = slice(128 * half, 128 * half + 128)
                send[base + 24 + 6 * half : base + 30 + 6 * half, :] = part_y[spot : spot + 6, lanes]
                send[base + 36 + 2 * half : base + 38 + 2 * half, :] = part_z[2 * rank : 2 * rank + 2, lanes]

    turned = lax.dot_general(
        q_terms[...], wyz[...], (((0,), (0,)), ((), ())), preferred_element_type=jnp.float32
    )
    turned = turned[0:128, :] + turned[128:256, :]
    mine[...] = jnp.where(gz == 0, turned[:, 0:128], turned[:, 128:256])
    theirs[...] = jnp.where(gz == 0, turned[:, 128:256], turned[:, 0:128])


def field(velocity, far, below, above, sides, omega_x, omega_y, omega_z, phi_x, phi_z):
    whole = pl.BlockSpec(memory_space=pltpu.VMEM)
    outside = pl.BlockSpec(memory_space=pl.ANY)
    half = jax.ShapeDtypeStruct((128, 128), jnp.float32)
    return pl.pallas_call(
        field_kernel,
        in_specs=[outside] * 13,
        out_specs=[whole] * 3,
        out_shape=[jax.ShapeDtypeStruct((1280, 128), jnp.float32), half, half],
        scratch_shapes=[
            pltpu.VMEM((3, 20, 112, 128), jnp.float32),
            pltpu.VMEM((3, 16, 96, 128), jnp.float32),
            pltpu.VMEM((2, 96, 128), jnp.float32),
            pltpu.VMEM((2, 3, 32, 128), jnp.float32),
            pltpu.VMEM((128, 256), jnp.int32),
            pltpu.VMEM((96, 256), jnp.int32),
            pltpu.VMEM((16, 256), jnp.int32),
            pltpu.VMEM((512, 128), jnp.int32),
            pltpu.VMEM((1536, 256), jnp.bfloat16),
            pltpu.VMEM((256, 128), jnp.float32),
            pltpu.VMEM((256, 256), jnp.bfloat16),
            pltpu.VMEM((256, 256), jnp.bfloat16),
            pltpu.VMEM((1536, 256), jnp.bfloat16),
            pltpu.VMEM((512, 256), jnp.bfloat16),
            pltpu.VMEM((96, 256), jnp.float32),
            pltpu.VMEM((16, 256), jnp.float32),
            pltpu.VMEM((2, 512, 128), jnp.float32),
            pltpu.SMEM((2, 16), jnp.int32),
            pltpu.SemaphoreType.DMA((14,)),
        ],
        compiler_params=pltpu.CompilerParams(vmem_limit_bytes=32 * 1024 * 1024),
        name="field_products",
    )(velocity, far, below, above, *sides, omega_x, omega_y, omega_z, phi_x, phi_z)


def split(values):
    high = lax.reduce_precision(values, 8, 7)
    return high.astype(jnp.bfloat16), (values - high).astype(jnp.bfloat16)


NEAR = [[4 * x + r for r in range(4)] for x in range(4)]


def gather(rows):
    return lax.all_gather(rows, "gx", axis=0, tiled=True, axis_index_groups=NEAR)


def pair_swap(rows):
    return lax.ppermute(rows, "gx", [(i, i ^ 4) for i in range(16)])


def cross_swap(rows):
    return lax.ppermute(rows, ("gx", "gz"), [(i, i ^ 9) for i in range(32)])


def unfold_kernel(own_y, beside_y, above_y, cross_y, own_z, beside_z, factor_y, factor_z):
    scale_y = 1.0 / math.sqrt(2048 * 32)
    scale_z = 1.0 / math.sqrt(2048 * 1536)
    gz = lax.axis_index("gz")
    pair = lax.rem(lax.axis_index("gx") // 4, 2)
    for x in range(2):
        rows_z = jnp.where(pair == x, own_z[...], beside_z[...]) * scale_z
        for z in range(2):
            near = jnp.where(gz == z, own_y[...], above_y[...])
            away = jnp.where(gz == z, beside_y[...], cross_y[...])
            rows_y = jnp.where(pair == x, near, away) * scale_y
            for r in range(4):
                rank = 4 * x + r
                spot = 6 * (2 * rank + z)
                factor_y[spot : spot + 6, 0:128] = rows_y[12 * r : 12 * r + 6, :]
                factor_y[spot : spot + 6, 128:256] = rows_y[12 * r + 6 : 12 * r + 12, :]
        for r in range(4):
            rank = 4 * x + r
            factor_z[2 * rank : 2 * rank + 2, 0:128] = rows_z[4 * r : 4 * r + 2, :]
            factor_z[2 * rank : 2 * rank + 2, 128:256] = rows_z[4 * r + 2 : 4 * r + 4, :]


def unfold(*pieces):
    whole = pl.BlockSpec(memory_space=pltpu.VMEM)
    return pl.pallas_call(
        unfold_kernel,
        in_specs=[whole] * 6,
        out_specs=[whole] * 2,
        out_shape=[jax.ShapeDtypeStruct((96, 256), jnp.float32), jax.ShapeDtypeStruct((16, 256), jnp.float32)],
        compiler_params=pltpu.CompilerParams(vmem_limit_bytes=4 * 1024 * 1024),
        cost_estimate=pl.CostEstimate(flops=0, bytes_accessed=0, transcendentals=0),
        name="unfold_factors",
    )(*pieces)


def exchange(rows, axes):
    return lax.all_to_all(rows, axes, 0, 0, tiled=True)


def shards(velocity, below, above, omega_x, omega_y, omega_z, phi_x, phi_y, phi_z):
    total_x = 2048
    total_y = 1536
    total_z = 32
    gz = lax.axis_index("gz")
    near, x_even, x_odd, y_even, y_odd = pack(velocity)
    far = shift_permute(near, "gz", 1)
    y_even = edge_swap(y_even, "gy", 0)
    y_odd = edge_swap(y_odd, "gy", 1)
    x_odd = edge_swap(x_odd, "gx", 1)
    x_even = edge_swap(x_even, "gx", 0)
    sides = [y_even, y_odd, x_odd, x_even]
    send, mine, theirs = field(velocity, far, below, above, sides, omega_x, omega_y, omega_z, phi_x, phi_z)
    got = exchange(send, ("gx", "gz")).reshape(16, 2, 40, 128)
    part_x = mine + shift_permute(theirs, "gz", 1)

    by_z = jnp.sum(got, axis=0)
    summed = by_z[0] + by_z[1]
    summed_z = jnp.where(gz == 0, by_z[0, 36:40], by_z[1, 36:40])
    rest = jnp.concatenate([summed[16:24, :64], summed[16:24, 64:]], axis=0)
    lead_high, lead_low = split(jnp.concatenate([summed[:16], rest], axis=1))
    wide = phi_y.T.astype(jnp.bfloat16)
    none = jnp.zeros((96, 512), jnp.bfloat16)
    wide = jnp.concatenate(
        [jnp.concatenate([wide, none], axis=1), jnp.concatenate([none, wide], axis=1)], axis=0
    )
    core = jnp.dot(jnp.concatenate([lead_high, lead_low], axis=0), wide, preferred_element_type=jnp.float32)
    core = (core[:16] + core[16:]).reshape(16, 8, 128)
    rows_z = jnp.broadcast_to(summed_z[None], (16, 4, 128))
    send = jnp.concatenate([core, part_x.reshape(16, 8, 128), rows_z], axis=1)
    got = jnp.sum(exchange(send.reshape(320, 128), "gy").reshape(16, 20, 128), axis=0)
    core_sketch = got[:8].reshape(1, 2, 512) * (1.0 / math.sqrt(total_x * total_y * total_z))

    own_y = gather(summed[24:36])
    pieces = (own_y, pair_swap(own_y), shift_permute(own_y, "gz", 1), cross_swap(own_y))
    rows, pieces = lax.optimization_barrier((got[8:20], pieces))
    got_x = exchange(jnp.broadcast_to(rows[None, :8], (32, 8, 128)).reshape(256, 128), ("gy", "gz"))
    own_z = gather(rows[8:])
    factor_y, factor_z = unfold(*pieces, own_z, pair_swap(own_z))

    factor_x = got_x.reshape(16, 2, 8, 128).transpose(0, 2, 1, 3).reshape(128, 256)
    factor_x = factor_x * (1.0 / math.sqrt(total_y * total_z))
    return (factor_x, factor_y, factor_z, core_sketch)


def solution(mesh):
    in_specs = (
        P(None, "gz", "gy", "gx"),
        P(None, None, "gy", "gx"),
        P(None, None, "gy", "gx"),
        P("gx", None),
        P("gy", None),
        P("gz", None),
        P(None, "gx"),
        P(None, "gy"),
        P(None, "gz"),
    )
    out_specs = (P("gx", None), P("gy", None), P("gz", None), P(("gx", "gy", "gz"), None, None))
    return jax.shard_map(shards, mesh=mesh, in_specs=in_specs, out_specs=out_specs, check_vma=False)
```

```python
import math

import jax
import jax.numpy as jnp
from jax import lax
from jax.experimental import pallas as pl
from jax.experimental.pallas import tpu as pltpu
from jax.sharding import PartitionSpec as P


def shift_permute(cells, axis, step):
    count = lax.axis_size(axis)
    return lax.ppermute(cells, axis, [(i, (i + step) % count) for i in range(count)])


def edge_swap(cells, axis, odd):
    count = lax.axis_size(axis)
    pairs = []
    for i in range(odd, count + odd, 2):
        pairs += [(i % count, (i + 1) % count), ((i + 1) % count, i % count)]
    return lax.ppermute(cells, axis, pairs)


def pack_kernel(vel, near, x_even, x_odd, y_even, y_odd):
    gz = lax.axis_index("gz")
    odd_x = lax.rem(lax.axis_index("gx"), 2) == 1
    odd_y = lax.rem(lax.axis_index("gy"), 2) == 1
    lane = lax.broadcasted_iota(jnp.int32, (96, 128), 1)
    high = jnp.zeros((96, 128), jnp.float32)
    low = jnp.zeros((96, 128), jnp.float32)
    for c in range(3):
        near[c] = vel[c, pl.ds(14 * (1 - gz), 2)]
        for k in range(16):
            spot = 2 * (16 * c + k)
            turned = pltpu.roll(vel[c, k], spot + 2, 1)
            high = jnp.where((lane >= spot) & (lane < spot + 2), turned, high)
            low = jnp.where((lane >= spot + 2) & (lane < spot + 4), turned, low)
            first = vel[c, k, 0:2, :]
            last = vel[c, k, 94:96, :]
            y_even[c, 2 * k : 2 * k + 2, :] = jnp.where(odd_y, first, last)
            y_odd[c, 2 * k : 2 * k + 2, :] = jnp.where(odd_y, last, first)
    x_even[...] = jnp.where(odd_x, low, high)
    x_odd[...] = jnp.where(odd_x, high, low)


def pack(velocity):
    rims = jax.ShapeDtypeStruct((96, 128), jnp.float32)
    rows = jax.ShapeDtypeStruct((3, 32, 128), jnp.float32)
    whole = pl.BlockSpec(memory_space=pltpu.VMEM)
    return pl.pallas_call(
        pack_kernel,
        in_specs=[whole],
        out_specs=[whole] * 5,
        out_shape=[jax.ShapeDtypeStruct((3, 2, 96, 128), jnp.float32), rims, rims, rows, rows],
        compiler_params=pltpu.CompilerParams(vmem_limit_bytes=32 * 1024 * 1024),
        name="pack_halos",
    )(velocity)


def field_kernel(
    vel, far, below, above, y_even, y_odd, x_odd, x_even, omega_x, omega_y, omega_z, phi_x, phi_z,
    send, part_x,
    padded, sides, x_held, y_held, wx_held, wy_held, wz_held, px_held,
    q_terms, flat, flat_terms, wx, wyz, phx, part_y, part_z, lead, pz_held, sems,
):
    gz = lax.axis_index("gz")
    odd_x = lax.rem(lax.axis_index("gx"), 2)
    odd_y = lax.rem(lax.axis_index("gy"), 2)
    middle = pl.ds(8, 96)
    x_copies = [
        pltpu.make_async_copy(x_even, x_held.at[1 - odd_x], sems.at[0]),
        pltpu.make_async_copy(x_odd, x_held.at[odd_x], sems.at[1]),
    ]
    y_copies = [
        pltpu.make_async_copy(y_even, y_held.at[1 - odd_y], sems.at[2]),
        pltpu.make_async_copy(y_odd, y_held.at[odd_y], sems.at[3]),
    ]
    cells_copies = [
        pltpu.make_async_copy(vel.at[c], padded.at[c, pl.ds(2, 16), middle, :], sems.at[4 + c]) for c in range(3)
    ]
    far_low = pltpu.make_async_copy(far, padded.at[:, pl.ds(0, 2), middle, :], sems.at[7])
    far_high = pltpu.make_async_copy(far, padded.at[:, pl.ds(18, 2), middle, :], sems.at[8])
    rim_low = pltpu.make_async_copy(below, padded.at[:, pl.ds(0, 2), middle, :], sems.at[7])
    rim_high = pltpu.make_async_copy(above, padded.at[:, pl.ds(18, 2), middle, :], sems.at[8])
    weight_copies = [
        pltpu.make_async_copy(omega_x, wx_held, sems.at[9]),
        pltpu.make_async_copy(omega_y, wy_held, sems.at[10]),
        pltpu.make_async_copy(omega_z, wz_held, sems.at[11]),
        pltpu.make_async_copy(phi_x, px_held, sems.at[12]),
    ]
    z_copy = pltpu.make_async_copy(phi_z, pz_held, sems.at[13])
    for copy in x_copies + cells_copies + y_copies + [z_copy]:
        copy.start()

    @pl.when(gz == 0)
    def _():
        rim_low.start()
        far_high.start()

    @pl.when(gz == 1)
    def _():
        far_low.start()
        rim_high.start()

    for copy in weight_copies:
        copy.start()
    for copy in x_copies:
        copy.wait()

    lane_all = lax.broadcasted_iota(jnp.int32, (96, 128), 1)

    def place(k, carry):
        for c in range(3):
            spot = 2 * (16 * c + k)
            both = jnp.where(lane_all < spot + 2, x_held[0], x_held[1])
            sides[c, k] = pltpu.roll(both, 126 - spot, 1)
        return carry

    lax.fori_loop(0, 16, place, 0, unroll=2)

    for copy in y_copies + cells_copies + [z_copy]:
        copy.wait()
    for c in range(3):
        for k in range(16):
            padded[c, k + 2, 6:8, :] = y_held[0, c, 2 * k : 2 * k + 2, :]
            padded[c, k + 2, 104:106, :] = y_held[1, c, 2 * k : 2 * k + 2, :]
    flat[...] = jnp.zeros((256, 128), jnp.float32)

    @pl.when(gz == 0)
    def _():
        rim_low.wait()
        far_high.wait()

    @pl.when(gz == 1)
    def _():
        far_low.wait()
        rim_high.wait()

    lane = lax.broadcasted_iota(jnp.int32, (16, 128), 1)

    def plane(k, carry):
        weight = [pz_held[c, k].astype(jnp.float32) for c in range(2)]
        for block in range(6):
            row = 16 * block
            at = row + 8
            along = [[], [], []]
            for c in range(3):
                cells = padded[c, k + 2, at : at + 16, :]
                rim = sides[c, k, row : row + 16, :]
                outer = pltpu.roll(jnp.where(lane >= 126, rim, cells), 2, 1) - pltpu.roll(
                    jnp.where(lane < 2, rim, cells), 126, 1
                )
                inner = pltpu.roll(jnp.where(lane < 1, rim, cells), 127, 1) - pltpu.roll(
                    jnp.where(lane >= 127, rim, cells), 1, 1
                )
                along[0].append(outer + 8.0 * inner)
                outer = padded[c, k + 2, at - 2 : at + 14, :] - padded[c, k + 2, at + 2 : at + 18, :]
                inner = padded[c, k + 2, at + 1 : at + 17, :] - padded[c, k + 2, at - 1 : at + 15, :]
                along[1].append(outer + 8.0 * inner)
                outer = padded[c, k, at : at + 16, :] - padded[c, k + 4, at : at + 16, :]
                inner = padded[c, k + 3, at : at + 16, :] - padded[c, k + 1, at : at + 16, :]
                along[2].append(outer + 8.0 * inner)
            diagonal = along[0][0] * along[0][0] + along[1][1] * along[1][1] + along[2][2] * along[2][2]
            mixed = along[0][1] * along[1][0] + along[0][2] * along[2][0] + along[1][2] * along[2][1]
            field = (-0.5 / 144.0) * (diagonal + 2.0 * mixed)
            high = field.astype(jnp.bfloat16)
            low = (field - high.astype(jnp.float32)).astype(jnp.bfloat16)
            rows = pl.ds(pl.multiple_of(96 * k + row, 16), 16)
            q_terms[rows, 0:128] = high
            q_terms[rows, 128:256] = low
            for c in range(2):
                flat[96 * c + row : 96 * c + row + 16, :] += weight[c] * field
        return carry

    lax.fori_loop(0, 16, plane, 0, unroll=4)

    for copy in weight_copies:
        copy.wait()
    wx[0:128, :] = wx_held[...].astype(jnp.float32).astype(jnp.bfloat16)
    wx[128:256, :] = wx_held[...].astype(jnp.float32).astype(jnp.bfloat16)
    phx[:, 0:128] = px_held[...].astype(jnp.float32).astype(jnp.bfloat16)
    phx[:, 128:256] = px_held[...].astype(jnp.float32).astype(jnp.bfloat16)
    wy = wy_held[...].astype(jnp.float32)
    wz = wz_held[...].astype(jnp.float32)

    flat_high = flat[...].astype(jnp.bfloat16)
    flat_terms[:, 0:128] = flat_high
    flat_terms[:, 128:256] = (flat[...] - flat_high.astype(jnp.float32)).astype(jnp.bfloat16)
    leading = lax.dot_general(
        phx[...], flat_terms[...], (((1,), (1,)), ((), ())), preferred_element_type=jnp.float32
    )
    lead[0] = leading[:, 0:128]
    lead[1] = leading[:, 128:256]

    total_y = jnp.zeros((96, 256), jnp.float32)
    for k in range(16):
        rows = slice(96 * k, 96 * k + 96)
        sums = jnp.dot(q_terms[rows, :], wx[...], preferred_element_type=jnp.float32)
        total_y = total_y + sums * wz[k : k + 1, :]
        part_z[k : k + 1, :] = jnp.sum(sums * wy, axis=0, keepdims=True)
        wyz[rows, :] = (wy * wz[k : k + 1, :]).astype(jnp.bfloat16)
    part_y[...] = total_y

    lane8 = lax.broadcasted_iota(jnp.int32, (8, 128), 1)
    for g in range(16):
        for z in range(2):
            chunk = 2 * g + z
            base = 40 * chunk
            near = 32 * g + z
            send[base : base + 16, :] = lead[0, pl.ds(near, 16, stride=2), :]
            send[base + 16 : base + 24, :] = jnp.where(
                lane8 < 64,
                lead[1, pl.ds(near, 8, stride=2), :],
                pltpu.roll(lead[1, pl.ds(near + 16, 8, stride=2), :], 64, 1),
            )
            rank = 4 * ((g // 4) % 2) + g % 4
            spot = 6 * (2 * rank + z)
            for half in range(2):
                lanes = slice(128 * half, 128 * half + 128)
                send[base + 24 + 6 * half : base + 30 + 6 * half, :] = part_y[spot : spot + 6, lanes]
                send[base + 36 + 2 * half : base + 38 + 2 * half, :] = part_z[2 * rank : 2 * rank + 2, lanes]

    turned = lax.dot_general(
        q_terms[...], wyz[...], (((0,), (0,)), ((), ())), preferred_element_type=jnp.float32
    )
    turned = turned[0:128, :] + turned[128:256, :]
    for h in range(16):
        part_x[16 * h : 16 * h + 8, :] = turned[8 * h : 8 * h + 8, 0:128]
        part_x[16 * h + 8 : 16 * h + 16, :] = turned[8 * h : 8 * h + 8, 128:256]


def field(velocity, far, below, above, sides, omega_x, omega_y, omega_z, phi_x, phi_z):
    whole = pl.BlockSpec(memory_space=pltpu.VMEM)
    outside = pl.BlockSpec(memory_space=pl.ANY)
    return pl.pallas_call(
        field_kernel,
        in_specs=[outside] * 13,
        out_specs=[whole] * 2,
        out_shape=[jax.ShapeDtypeStruct((1280, 128), jnp.float32), jax.ShapeDtypeStruct((256, 128), jnp.float32)],
        scratch_shapes=[
            pltpu.VMEM((3, 20, 112, 128), jnp.float32),
            pltpu.VMEM((3, 16, 96, 128), jnp.float32),
            pltpu.VMEM((2, 96, 128), jnp.float32),
            pltpu.VMEM((2, 3, 32, 128), jnp.float32),
            pltpu.VMEM((128, 256), jnp.int32),
            pltpu.VMEM((96, 256), jnp.int32),
            pltpu.VMEM((16, 256), jnp.int32),
            pltpu.VMEM((512, 128), jnp.int32),
            pltpu.VMEM((1536, 256), jnp.bfloat16),
            pltpu.VMEM((256, 128), jnp.float32),
            pltpu.VMEM((256, 256), jnp.bfloat16),
            pltpu.VMEM((256, 256), jnp.bfloat16),
            pltpu.VMEM((1536, 256), jnp.bfloat16),
            pltpu.VMEM((512, 256), jnp.bfloat16),
            pltpu.VMEM((96, 256), jnp.float32),
            pltpu.VMEM((16, 256), jnp.float32),
            pltpu.VMEM((2, 512, 128), jnp.float32),
            pltpu.SMEM((2, 16), jnp.int32),
            pltpu.SemaphoreType.DMA((14,)),
        ],
        compiler_params=pltpu.CompilerParams(vmem_limit_bytes=32 * 1024 * 1024),
        name="field_products",
    )(velocity, far, below, above, *sides, omega_x, omega_y, omega_z, phi_x, phi_z)


def split(values):
    high = lax.reduce_precision(values, 8, 7)
    return high.astype(jnp.bfloat16), (values - high).astype(jnp.bfloat16)


NEAR = [[4 * x + r for r in range(4)] for x in range(4)]


def gather(rows):
    return lax.all_gather(rows, "gx", axis=0, tiled=True, axis_index_groups=NEAR)


def pair_swap(rows):
    return lax.ppermute(rows, "gx", [(i, i ^ 4) for i in range(16)])


def cross_swap(rows):
    return lax.ppermute(rows, ("gx", "gz"), [(i, i ^ 9) for i in range(32)])


def unfold_kernel(own_y, beside_y, above_y, cross_y, own_z, beside_z, factor_y, factor_z):
    scale_y = 1.0 / math.sqrt(2048 * 32)
    scale_z = 1.0 / math.sqrt(2048 * 1536)
    gz = lax.axis_index("gz")
    pair = lax.rem(lax.axis_index("gx") // 4, 2)
    for x in range(2):
        rows_z = jnp.where(pair == x, own_z[...], beside_z[...]) * scale_z
        for z in range(2):
            near = jnp.where(gz == z, own_y[...], above_y[...])
            away = jnp.where(gz == z, beside_y[...], cross_y[...])
            rows_y = jnp.where(pair == x, near, away) * scale_y
            for r in range(4):
                rank = 4 * x + r
                spot = 6 * (2 * rank + z)
                factor_y[spot : spot + 6, 0:128] = rows_y[12 * r : 12 * r + 6, :]
                factor_y[spot : spot + 6, 128:256] = rows_y[12 * r + 6 : 12 * r + 12, :]
        for r in range(4):
            rank = 4 * x + r
            factor_z[2 * rank : 2 * rank + 2, 0:128] = rows_z[4 * r : 4 * r + 2, :]
            factor_z[2 * rank : 2 * rank + 2, 128:256] = rows_z[4 * r + 2 : 4 * r + 4, :]


def unfold(*pieces):
    whole = pl.BlockSpec(memory_space=pltpu.VMEM)
    return pl.pallas_call(
        unfold_kernel,
        in_specs=[whole] * 6,
        out_specs=[whole] * 2,
        out_shape=[jax.ShapeDtypeStruct((96, 256), jnp.float32), jax.ShapeDtypeStruct((16, 256), jnp.float32)],
        compiler_params=pltpu.CompilerParams(vmem_limit_bytes=4 * 1024 * 1024),
        cost_estimate=pl.CostEstimate(flops=0, bytes_accessed=0, transcendentals=0),
        name="unfold_factors",
    )(*pieces)


def exchange(rows, axes):
    return lax.all_to_all(rows, axes, 0, 0, tiled=True)


def shards(velocity, below, above, omega_x, omega_y, omega_z, phi_x, phi_y, phi_z):
    total_x = 2048
    total_y = 1536
    total_z = 32
    gz = lax.axis_index("gz")
    near, x_even, x_odd, y_even, y_odd = pack(velocity)
    far = shift_permute(near, "gz", 1)
    y_even = edge_swap(y_even, "gy", 0)
    y_odd = edge_swap(y_odd, "gy", 1)
    x_odd = edge_swap(x_odd, "gx", 1)
    x_even = edge_swap(x_even, "gx", 0)
    sides = [y_even, y_odd, x_odd, x_even]
    send, part_x = field(velocity, far, below, above, sides, omega_x, omega_y, omega_z, phi_x, phi_z)
    got = exchange(send, ("gx", "gz")).reshape(16, 2, 40, 128)
    part_x = part_x + shift_permute(part_x, "gz", 1)

    by_z = jnp.sum(got, axis=0)
    summed = by_z[0] + by_z[1]
    summed_z = jnp.where(gz == 0, by_z[0, 36:40], by_z[1, 36:40])
    rest = jnp.concatenate([summed[16:24, :64], summed[16:24, 64:]], axis=0)
    lead_high, lead_low = split(jnp.concatenate([summed[:16], rest], axis=1))
    wide = phi_y.T.astype(jnp.bfloat16)
    none = jnp.zeros((96, 512), jnp.bfloat16)
    wide = jnp.concatenate(
        [jnp.concatenate([wide, none], axis=1), jnp.concatenate([none, wide], axis=1)], axis=0
    )
    core = jnp.dot(jnp.concatenate([lead_high, lead_low], axis=0), wide, preferred_element_type=jnp.float32)
    core = (core[:16] + core[16:]).reshape(16, 8, 128)
    rows_z = jnp.broadcast_to(summed_z[None], (16, 4, 128))
    send = jnp.concatenate([core, part_x.reshape(16, 16, 128), rows_z], axis=1)
    got = jnp.sum(exchange(send.reshape(16, 7, 4, 128), "gy"), axis=0).reshape(28, 128)
    core_sketch = got[:8].reshape(1, 2, 512) * (1.0 / math.sqrt(total_x * total_y * total_z))

    own_y = gather(summed[24:36])
    cross_y = cross_swap(own_y)
    rows, own_y, beside_y, above_y = lax.optimization_barrier(
        (got[8:28], own_y, pair_swap(own_y), shift_permute(own_y, "gz", 1))
    )
    got_x = exchange(jnp.broadcast_to(rows[None, :16], (16, 16, 128)).reshape(256, 128), "gy")
    own_z = gather(rows[16:])
    factor_y, factor_z = unfold(own_y, beside_y, above_y, cross_y, own_z, pair_swap(own_z))

    factor_x = got_x.reshape(16, 2, 8, 128).transpose(0, 2, 1, 3).reshape(128, 256)
    factor_x = factor_x * (1.0 / math.sqrt(total_y * total_z))
    return (factor_x, factor_y, factor_z, core_sketch)


def solution(mesh):
    in_specs = (
        P(None, "gz", "gy", "gx"),
        P(None, None, "gy", "gx"),
        P(None, None, "gy", "gx"),
        P("gx", None),
        P("gy", None),
        P("gz", None),
        P(None, "gx"),
        P(None, "gy"),
        P(None, "gz"),
    )
    out_specs = (P("gx", None), P("gy", None), P("gz", None), P(("gx", "gy", "gz"), None, None))
    return jax.shard_map(shards, mesh=mesh, in_specs=in_specs, out_specs=out_specs, check_vma=False)
```

```python
import math

import jax
import jax.numpy as jnp
from jax import lax
from jax.experimental import pallas as pl
from jax.experimental.pallas import tpu as pltpu
from jax.sharding import PartitionSpec as P


def shift_permute(cells, axis, step):
    count = lax.axis_size(axis)
    return lax.ppermute(cells, axis, [(i, (i + step) % count) for i in range(count)])


def edge_swap(cells, axis, odd):
    count = lax.axis_size(axis)
    pairs = []
    for i in range(odd, count + odd, 2):
        pairs += [(i % count, (i + 1) % count), ((i + 1) % count, i % count)]
    return lax.ppermute(cells, axis, pairs)


def pack_kernel(vel, near, x_even, x_odd, y_even, y_odd):
    gz = lax.axis_index("gz")
    odd_x = lax.rem(lax.axis_index("gx"), 2) == 1
    odd_y = lax.rem(lax.axis_index("gy"), 2) == 1
    lane = lax.broadcasted_iota(jnp.int32, (96, 128), 1)
    high = jnp.zeros((96, 128), jnp.float32)
    low = jnp.zeros((96, 128), jnp.float32)
    for c in range(3):
        near[c] = vel[c, pl.ds(14 * (1 - gz), 2)]
        for k in range(16):
            spot = 2 * (16 * c + k)
            turned = pltpu.roll(vel[c, k], spot + 2, 1)
            high = jnp.where((lane >= spot) & (lane < spot + 2), turned, high)
            low = jnp.where((lane >= spot + 2) & (lane < spot + 4), turned, low)
            first = vel[c, k, 0:2, :]
            last = vel[c, k, 94:96, :]
            y_even[c, 2 * k : 2 * k + 2, :] = jnp.where(odd_y, first, last)
            y_odd[c, 2 * k : 2 * k + 2, :] = jnp.where(odd_y, last, first)
    x_even[...] = jnp.where(odd_x, low, high)
    x_odd[...] = jnp.where(odd_x, high, low)


def pack(velocity):
    rims = jax.ShapeDtypeStruct((96, 128), jnp.float32)
    rows = jax.ShapeDtypeStruct((3, 32, 128), jnp.float32)
    whole = pl.BlockSpec(memory_space=pltpu.VMEM)
    return pl.pallas_call(
        pack_kernel,
        in_specs=[whole],
        out_specs=[whole] * 5,
        out_shape=[jax.ShapeDtypeStruct((3, 2, 96, 128), jnp.float32), rims, rims, rows, rows],
        compiler_params=pltpu.CompilerParams(vmem_limit_bytes=32 * 1024 * 1024),
        name="pack_halos",
    )(velocity)


def field_kernel(
    vel, far, below, above, y_even, y_odd, x_odd, x_even, omega_x, omega_y, omega_z, phi_x, phi_z,
    send, part_x,
    padded, sides, x_held, y_held, wx_held, wy_held, wz_held, px_held,
    q_terms, flat, flat_terms, wx, wyz, phx, part_y, part_z, lead, pz_held, sems,
):
    gz = lax.axis_index("gz")
    odd_x = lax.rem(lax.axis_index("gx"), 2)
    odd_y = lax.rem(lax.axis_index("gy"), 2)
    middle = pl.ds(8, 96)
    x_copies = [
        pltpu.make_async_copy(x_even, x_held.at[1 - odd_x], sems.at[0]),
        pltpu.make_async_copy(x_odd, x_held.at[odd_x], sems.at[1]),
    ]
    y_copies = [
        pltpu.make_async_copy(y_even, y_held.at[1 - odd_y], sems.at[2]),
        pltpu.make_async_copy(y_odd, y_held.at[odd_y], sems.at[3]),
    ]
    cells_copies = [
        pltpu.make_async_copy(vel.at[c], padded.at[c, pl.ds(2, 16), middle, :], sems.at[4 + c]) for c in range(3)
    ]
    far_low = pltpu.make_async_copy(far, padded.at[:, pl.ds(0, 2), middle, :], sems.at[7])
    far_high = pltpu.make_async_copy(far, padded.at[:, pl.ds(18, 2), middle, :], sems.at[8])
    rim_low = pltpu.make_async_copy(below, padded.at[:, pl.ds(0, 2), middle, :], sems.at[7])
    rim_high = pltpu.make_async_copy(above, padded.at[:, pl.ds(18, 2), middle, :], sems.at[8])
    weight_copies = [
        pltpu.make_async_copy(omega_x, wx_held, sems.at[9]),
        pltpu.make_async_copy(omega_y, wy_held, sems.at[10]),
        pltpu.make_async_copy(omega_z, wz_held, sems.at[11]),
        pltpu.make_async_copy(phi_x, px_held, sems.at[12]),
    ]
    z_copy = pltpu.make_async_copy(phi_z, pz_held, sems.at[13])
    for copy in x_copies + cells_copies + y_copies + [z_copy]:
        copy.start()

    @pl.when(gz == 0)
    def _():
        rim_low.start()
        far_high.start()

    @pl.when(gz == 1)
    def _():
        far_low.start()
        rim_high.start()

    for copy in weight_copies:
        copy.start()
    for copy in x_copies:
        copy.wait()

    lane_all = lax.broadcasted_iota(jnp.int32, (96, 128), 1)

    def place(k, carry):
        for c in range(3):
            spot = 2 * (16 * c + k)
            both = jnp.where(lane_all < spot + 2, x_held[0], x_held[1])
            sides[c, k] = pltpu.roll(both, 126 - spot, 1)
        return carry

    lax.fori_loop(0, 16, place, 0, unroll=2)

    for copy in y_copies + cells_copies + [z_copy]:
        copy.wait()
    for c in range(3):
        for k in range(16):
            padded[c, k + 2, 6:8, :] = y_held[0, c, 2 * k : 2 * k + 2, :]
            padded[c, k + 2, 104:106, :] = y_held[1, c, 2 * k : 2 * k + 2, :]
    flat[...] = jnp.zeros((256, 128), jnp.float32)

    @pl.when(gz == 0)
    def _():
        rim_low.wait()
        far_high.wait()

    @pl.when(gz == 1)
    def _():
        far_low.wait()
        rim_high.wait()

    lane = lax.broadcasted_iota(jnp.int32, (16, 128), 1)

    def plane(k, carry):
        weight = [pz_held[c, k].astype(jnp.float32) for c in range(2)]
        for block in range(6):
            row = 16 * block
            at = row + 8
            along = [[], [], []]
            for c in range(3):
                cells = padded[c, k + 2, at : at + 16, :]
                rim = sides[c, k, row : row + 16, :]
                outer = pltpu.roll(jnp.where(lane >= 126, rim, cells), 2, 1) - pltpu.roll(
                    jnp.where(lane < 2, rim, cells), 126, 1
                )
                inner = pltpu.roll(jnp.where(lane < 1, rim, cells), 127, 1) - pltpu.roll(
                    jnp.where(lane >= 127, rim, cells), 1, 1
                )
                along[0].append(outer + 8.0 * inner)
                outer = padded[c, k + 2, at - 2 : at + 14, :] - padded[c, k + 2, at + 2 : at + 18, :]
                inner = padded[c, k + 2, at + 1 : at + 17, :] - padded[c, k + 2, at - 1 : at + 15, :]
                along[1].append(outer + 8.0 * inner)
                outer = padded[c, k, at : at + 16, :] - padded[c, k + 4, at : at + 16, :]
                inner = padded[c, k + 3, at : at + 16, :] - padded[c, k + 1, at : at + 16, :]
                along[2].append(outer + 8.0 * inner)
            diagonal = along[0][0] * along[0][0] + along[1][1] * along[1][1] + along[2][2] * along[2][2]
            mixed = along[0][1] * along[1][0] + along[0][2] * along[2][0] + along[1][2] * along[2][1]
            field = (-0.5 / 144.0) * (diagonal + 2.0 * mixed)
            high = field.astype(jnp.bfloat16)
            low = (field - high.astype(jnp.float32)).astype(jnp.bfloat16)
            rows = pl.ds(pl.multiple_of(96 * k + row, 16), 16)
            q_terms[rows, 0:128] = high
            q_terms[rows, 128:256] = low
            for c in range(2):
                flat[96 * c + row : 96 * c + row + 16, :] += weight[c] * field
        return carry

    lax.fori_loop(0, 16, plane, 0, unroll=4)

    for copy in weight_copies:
        copy.wait()
    wx[0:128, :] = wx_held[...].astype(jnp.float32).astype(jnp.bfloat16)
    wx[128:256, :] = wx_held[...].astype(jnp.float32).astype(jnp.bfloat16)
    phx[:, 0:128] = px_held[...].astype(jnp.float32).astype(jnp.bfloat16)
    phx[:, 128:256] = px_held[...].astype(jnp.float32).astype(jnp.bfloat16)
    wy = wy_held[...].astype(jnp.float32)
    wz = wz_held[...].astype(jnp.float32)

    flat_high = flat[...].astype(jnp.bfloat16)
    flat_terms[:, 0:128] = flat_high
    flat_terms[:, 128:256] = (flat[...] - flat_high.astype(jnp.float32)).astype(jnp.bfloat16)
    leading = lax.dot_general(
        phx[...], flat_terms[...], (((1,), (1,)), ((), ())), preferred_element_type=jnp.float32
    )
    lead[0] = leading[:, 0:128]
    lead[1] = leading[:, 128:256]

    total_y = jnp.zeros((96, 256), jnp.float32)
    for k in range(16):
        rows = slice(96 * k, 96 * k + 96)
        sums = jnp.dot(q_terms[rows, :], wx[...], preferred_element_type=jnp.float32)
        total_y = total_y + sums * wz[k : k + 1, :]
        part_z[k : k + 1, :] = jnp.sum(sums * wy, axis=0, keepdims=True)
        wyz[rows, :] = (wy * wz[k : k + 1, :]).astype(jnp.bfloat16)
    part_y[...] = total_y

    lane8 = lax.broadcasted_iota(jnp.int32, (8, 128), 1)
    for g in range(16):
        for z in range(2):
            chunk = 2 * g + z
            base = 40 * chunk
            near = 32 * g + z
            send[base : base + 16, :] = lead[0, pl.ds(near, 16, stride=2), :]
            send[base + 16 : base + 24, :] = jnp.where(
                lane8 < 64,
                lead[1, pl.ds(near, 8, stride=2), :],
                pltpu.roll(lead[1, pl.ds(near + 16, 8, stride=2), :], 64, 1),
            )
            rank = 4 * ((g // 4) % 2) + g % 4
            spot = 6 * (2 * rank + z)
            for half in range(2):
                lanes = slice(128 * half, 128 * half + 128)
                send[base + 24 + 6 * half : base + 30 + 6 * half, :] = part_y[spot : spot + 6, lanes]
                send[base + 36 + 2 * half : base + 38 + 2 * half, :] = part_z[2 * rank : 2 * rank + 2, lanes]

    turned = lax.dot_general(
        q_terms[...], wyz[...], (((0,), (0,)), ((), ())), preferred_element_type=jnp.float32
    )
    turned = turned[0:128, :] + turned[128:256, :]
    for h in range(16):
        part_x[16 * h : 16 * h + 8, :] = turned[8 * h : 8 * h + 8, 0:128]
        part_x[16 * h + 8 : 16 * h + 16, :] = turned[8 * h : 8 * h + 8, 128:256]


def field(velocity, far, below, above, sides, omega_x, omega_y, omega_z, phi_x, phi_z):
    whole = pl.BlockSpec(memory_space=pltpu.VMEM)
    outside = pl.BlockSpec(memory_space=pl.ANY)
    return pl.pallas_call(
        field_kernel,
        in_specs=[outside] * 13,
        out_specs=[whole] * 2,
        out_shape=[jax.ShapeDtypeStruct((1280, 128), jnp.float32), jax.ShapeDtypeStruct((256, 128), jnp.float32)],
        scratch_shapes=[
            pltpu.VMEM((3, 20, 112, 128), jnp.float32),
            pltpu.VMEM((3, 16, 96, 128), jnp.float32),
            pltpu.VMEM((2, 96, 128), jnp.float32),
            pltpu.VMEM((2, 3, 32, 128), jnp.float32),
            pltpu.VMEM((128, 256), jnp.int32),
            pltpu.VMEM((96, 256), jnp.int32),
            pltpu.VMEM((16, 256), jnp.int32),
            pltpu.VMEM((512, 128), jnp.int32),
            pltpu.VMEM((1536, 256), jnp.bfloat16),
            pltpu.VMEM((256, 128), jnp.float32),
            pltpu.VMEM((256, 256), jnp.bfloat16),
            pltpu.VMEM((256, 256), jnp.bfloat16),
            pltpu.VMEM((1536, 256), jnp.bfloat16),
            pltpu.VMEM((512, 256), jnp.bfloat16),
            pltpu.VMEM((96, 256), jnp.float32),
            pltpu.VMEM((16, 256), jnp.float32),
            pltpu.VMEM((2, 512, 128), jnp.float32),
            pltpu.SMEM((2, 16), jnp.int32),
            pltpu.SemaphoreType.DMA((14,)),
        ],
        compiler_params=pltpu.CompilerParams(vmem_limit_bytes=32 * 1024 * 1024),
        name="field_products",
    )(velocity, far, below, above, *sides, omega_x, omega_y, omega_z, phi_x, phi_z)


def split(values):
    high = lax.reduce_precision(values, 8, 7)
    return high.astype(jnp.bfloat16), (values - high).astype(jnp.bfloat16)


NEAR = [[4 * x + r for r in range(4)] for x in range(4)]


def gather(rows):
    return lax.all_gather(rows, "gx", axis=0, tiled=True, axis_index_groups=NEAR)


def pair_swap(rows):
    return lax.ppermute(rows, "gx", [(i, i ^ 4) for i in range(16)])


def unfold_kernel(both_y, beside_y, own_z, beside_z, factor_y, factor_z):
    scale_y = 1.0 / math.sqrt(2048 * 32)
    scale_z = 1.0 / math.sqrt(2048 * 1536)
    gz = lax.axis_index("gz")
    pair = lax.rem(lax.axis_index("gx") // 4, 2)
    for x in range(2):
        rows_z = jnp.where(pair == x, own_z[...], beside_z[...]) * scale_z
        for z in range(2):
            near = jnp.where(gz == z, both_y[0:48, :], both_y[48:96, :])
            away = jnp.where(gz == z, beside_y[0:48, :], beside_y[48:96, :])
            rows_y = jnp.where(pair == x, near, away) * scale_y
            for r in range(4):
                rank = 4 * x + r
                spot = 6 * (2 * rank + z)
                factor_y[spot : spot + 6, 0:128] = rows_y[12 * r : 12 * r + 6, :]
                factor_y[spot : spot + 6, 128:256] = rows_y[12 * r + 6 : 12 * r + 12, :]
        for r in range(4):
            rank = 4 * x + r
            factor_z[2 * rank : 2 * rank + 2, 0:128] = rows_z[4 * r : 4 * r + 2, :]
            factor_z[2 * rank : 2 * rank + 2, 128:256] = rows_z[4 * r + 2 : 4 * r + 4, :]


def unfold(*pieces):
    whole = pl.BlockSpec(memory_space=pltpu.VMEM)
    return pl.pallas_call(
        unfold_kernel,
        in_specs=[whole] * 4,
        out_specs=[whole] * 2,
        out_shape=[jax.ShapeDtypeStruct((96, 256), jnp.float32), jax.ShapeDtypeStruct((16, 256), jnp.float32)],
        compiler_params=pltpu.CompilerParams(vmem_limit_bytes=4 * 1024 * 1024),
        cost_estimate=pl.CostEstimate(flops=0, bytes_accessed=0, transcendentals=0),
        name="unfold_factors",
    )(*pieces)


def exchange(rows, axes):
    return lax.all_to_all(rows, axes, 0, 0, tiled=True)


def shards(velocity, below, above, omega_x, omega_y, omega_z, phi_x, phi_y, phi_z):
    total_x = 2048
    total_y = 1536
    total_z = 32
    gz = lax.axis_index("gz")
    near, x_even, x_odd, y_even, y_odd = pack(velocity)
    far = shift_permute(near, "gz", 1)
    y_even = edge_swap(y_even, "gy", 0)
    y_odd = edge_swap(y_odd, "gy", 1)
    x_odd = edge_swap(x_odd, "gx", 1)
    x_even = edge_swap(x_even, "gx", 0)
    sides = [y_even, y_odd, x_odd, x_even]
    send, part_x = field(velocity, far, below, above, sides, omega_x, omega_y, omega_z, phi_x, phi_z)
    got = exchange(send, ("gx", "gz")).reshape(16, 2, 40, 128)
    part_x = part_x + shift_permute(part_x, "gz", 1)

    by_z = jnp.sum(got, axis=0)
    summed = by_z[0] + by_z[1]
    summed_z = jnp.where(gz == 0, by_z[0, 36:40], by_z[1, 36:40])
    rest = jnp.concatenate([summed[16:24, :64], summed[16:24, 64:]], axis=0)
    lead_high, lead_low = split(jnp.concatenate([summed[:16], rest], axis=1))
    wide = phi_y.T.astype(jnp.bfloat16)
    none = jnp.zeros((96, 512), jnp.bfloat16)
    wide = jnp.concatenate(
        [jnp.concatenate([wide, none], axis=1), jnp.concatenate([none, wide], axis=1)], axis=0
    )
    core = jnp.dot(jnp.concatenate([lead_high, lead_low], axis=0), wide, preferred_element_type=jnp.float32)
    core = (core[:16] + core[16:]).reshape(16, 8, 128)
    rows_z = jnp.broadcast_to(summed_z[None], (16, 4, 128))
    send = jnp.concatenate([core, part_x.reshape(16, 16, 128), rows_z], axis=1)
    got = jnp.sum(exchange(send.reshape(16, 7, 4, 128), "gy"), axis=0).reshape(28, 128)
    core_sketch = got[:8].reshape(1, 2, 512) * (1.0 / math.sqrt(total_x * total_y * total_z))

    own_y = gather(summed[24:36])
    both_y = jnp.concatenate([own_y, shift_permute(own_y, "gz", 1)], axis=0)
    rows, both_y, beside_y = lax.optimization_barrier((got[8:28], both_y, pair_swap(both_y)))
    got_x = exchange(jnp.broadcast_to(rows[None, :16], (16, 16, 128)).reshape(256, 128), "gy")
    own_z = gather(rows[16:])
    factor_y, factor_z = unfold(both_y, beside_y, own_z, pair_swap(own_z))

    factor_x = got_x.reshape(16, 2, 8, 128).transpose(0, 2, 1, 3).reshape(128, 256)
    factor_x = factor_x * (1.0 / math.sqrt(total_y * total_z))
    return (factor_x, factor_y, factor_z, core_sketch)


def solution(mesh):
    in_specs = (
        P(None, "gz", "gy", "gx"),
        P(None, None, "gy", "gx"),
        P(None, None, "gy", "gx"),
        P("gx", None),
        P("gy", None),
        P("gz", None),
        P(None, "gx"),
        P(None, "gy"),
        P(None, "gz"),
    )
    out_specs = (P("gx", None), P("gy", None), P("gz", None), P(("gx", "gy", "gz"), None, None))
    return jax.shard_map(shards, mesh=mesh, in_specs=in_specs, out_specs=out_specs, check_vma=False)
```

```python
import math

import jax
import jax.numpy as jnp
from jax import lax
from jax.experimental import pallas as pl
from jax.experimental.pallas import tpu as pltpu
from jax.sharding import PartitionSpec as P


def shift_permute(cells, axis, step):
    count = lax.axis_size(axis)
    return lax.ppermute(cells, axis, [(i, (i + step) % count) for i in range(count)])


def edge_swap(cells, axis, odd):
    count = lax.axis_size(axis)
    pairs = []
    for i in range(odd, count + odd, 2):
        pairs += [(i % count, (i + 1) % count), ((i + 1) % count, i % count)]
    return lax.ppermute(cells, axis, pairs)


def pack_kernel(vel, near, x_even, x_odd, y_even, y_odd):
    gz = lax.axis_index("gz")
    odd_x = lax.rem(lax.axis_index("gx"), 2) == 1
    odd_y = lax.rem(lax.axis_index("gy"), 2) == 1
    lane = lax.broadcasted_iota(jnp.int32, (96, 128), 1)
    high = jnp.zeros((96, 128), jnp.float32)
    low = jnp.zeros((96, 128), jnp.float32)
    for c in range(3):
        near[c] = vel[c, pl.ds(14 * (1 - gz), 2)]
        for k in range(16):
            spot = 2 * (16 * c + k)
            turned = pltpu.roll(vel[c, k], spot + 2, 1)
            high = jnp.where((lane >= spot) & (lane < spot + 2), turned, high)
            low = jnp.where((lane >= spot + 2) & (lane < spot + 4), turned, low)
            first = vel[c, k, 0:2, :]
            last = vel[c, k, 94:96, :]
            y_even[c, 2 * k : 2 * k + 2, :] = jnp.where(odd_y, first, last)
            y_odd[c, 2 * k : 2 * k + 2, :] = jnp.where(odd_y, last, first)
    x_even[...] = jnp.where(odd_x, low, high)
    x_odd[...] = jnp.where(odd_x, high, low)


def pack(velocity):
    rims = jax.ShapeDtypeStruct((96, 128), jnp.float32)
    rows = jax.ShapeDtypeStruct((3, 32, 128), jnp.float32)
    whole = pl.BlockSpec(memory_space=pltpu.VMEM)
    return pl.pallas_call(
        pack_kernel,
        in_specs=[whole],
        out_specs=[whole] * 5,
        out_shape=[jax.ShapeDtypeStruct((3, 2, 96, 128), jnp.float32), rims, rims, rows, rows],
        compiler_params=pltpu.CompilerParams(vmem_limit_bytes=32 * 1024 * 1024),
        name="pack_halos",
    )(velocity)


def field_kernel(
    vel, far, below, above, y_even, y_odd, x_odd, x_even, omega_x, omega_y, omega_z, phi_x, phi_z,
    send, part_x,
    padded, sides, x_held, y_held, wx_held, wy_held, wz_held, px_held,
    q_terms, flat, flat_terms, wx, wyz, phx, part_y, part_z, lead, pz_held, sems,
):
    gz = lax.axis_index("gz")
    odd_x = lax.rem(lax.axis_index("gx"), 2)
    odd_y = lax.rem(lax.axis_index("gy"), 2)
    middle = pl.ds(8, 96)
    x_copies = [
        pltpu.make_async_copy(x_even, x_held.at[1 - odd_x], sems.at[0]),
        pltpu.make_async_copy(x_odd, x_held.at[odd_x], sems.at[1]),
    ]
    y_copies = [
        pltpu.make_async_copy(y_even, y_held.at[1 - odd_y], sems.at[2]),
        pltpu.make_async_copy(y_odd, y_held.at[odd_y], sems.at[3]),
    ]
    cells_copies = [
        pltpu.make_async_copy(vel.at[c], padded.at[c, pl.ds(2, 16), middle, :], sems.at[4 + c]) for c in range(3)
    ]
    far_low = pltpu.make_async_copy(far, padded.at[:, pl.ds(0, 2), middle, :], sems.at[7])
    far_high = pltpu.make_async_copy(far, padded.at[:, pl.ds(18, 2), middle, :], sems.at[8])
    rim_low = pltpu.make_async_copy(below, padded.at[:, pl.ds(0, 2), middle, :], sems.at[7])
    rim_high = pltpu.make_async_copy(above, padded.at[:, pl.ds(18, 2), middle, :], sems.at[8])
    weight_copies = [
        pltpu.make_async_copy(omega_x, wx_held, sems.at[9]),
        pltpu.make_async_copy(omega_y, wy_held, sems.at[10]),
        pltpu.make_async_copy(omega_z, wz_held, sems.at[11]),
        pltpu.make_async_copy(phi_x, px_held, sems.at[12]),
    ]
    z_copy = pltpu.make_async_copy(phi_z, pz_held, sems.at[13])
    for copy in x_copies + cells_copies + y_copies + [z_copy]:
        copy.start()

    @pl.when(gz == 0)
    def _():
        rim_low.start()
        far_high.start()

    @pl.when(gz == 1)
    def _():
        far_low.start()
        rim_high.start()

    for copy in weight_copies:
        copy.start()
    for copy in x_copies:
        copy.wait()

    lane_all = lax.broadcasted_iota(jnp.int32, (96, 128), 1)

    def place(k, carry):
        for c in range(3):
            spot = 2 * (16 * c + k)
            both = jnp.where(lane_all < spot + 2, x_held[0], x_held[1])
            sides[c, k] = pltpu.roll(both, 126 - spot, 1)
        return carry

    lax.fori_loop(0, 16, place, 0, unroll=2)

    for copy in y_copies + cells_copies + [z_copy]:
        copy.wait()
    for c in range(3):
        for k in range(16):
            padded[c, k + 2, 6:8, :] = y_held[0, c, 2 * k : 2 * k + 2, :]
            padded[c, k + 2, 104:106, :] = y_held[1, c, 2 * k : 2 * k + 2, :]
    flat[...] = jnp.zeros((256, 128), jnp.float32)

    @pl.when(gz == 0)
    def _():
        rim_low.wait()
        far_high.wait()

    @pl.when(gz == 1)
    def _():
        far_low.wait()
        rim_high.wait()

    lane = lax.broadcasted_iota(jnp.int32, (16, 128), 1)

    def plane(k, carry):
        weight = [pz_held[c, k].astype(jnp.float32) for c in range(2)]
        for block in range(6):
            row = 16 * block
            at = row + 8
            along = [[], [], []]
            for c in range(3):
                cells = padded[c, k + 2, at : at + 16, :]
                rim = sides[c, k, row : row + 16, :]
                outer = pltpu.roll(jnp.where(lane >= 126, rim, cells), 2, 1) - pltpu.roll(
                    jnp.where(lane < 2, rim, cells), 126, 1
                )
                inner = pltpu.roll(jnp.where(lane < 1, rim, cells), 127, 1) - pltpu.roll(
                    jnp.where(lane >= 127, rim, cells), 1, 1
                )
                along[0].append(outer + 8.0 * inner)
                outer = padded[c, k + 2, at - 2 : at + 14, :] - padded[c, k + 2, at + 2 : at + 18, :]
                inner = padded[c, k + 2, at + 1 : at + 17, :] - padded[c, k + 2, at - 1 : at + 15, :]
                along[1].append(outer + 8.0 * inner)
                outer = padded[c, k, at : at + 16, :] - padded[c, k + 4, at : at + 16, :]
                inner = padded[c, k + 3, at : at + 16, :] - padded[c, k + 1, at : at + 16, :]
                along[2].append(outer + 8.0 * inner)
            diagonal = along[0][0] * along[0][0] + along[1][1] * along[1][1] + along[2][2] * along[2][2]
            mixed = along[0][1] * along[1][0] + along[0][2] * along[2][0] + along[1][2] * along[2][1]
            field = (-0.5 / 144.0) * (diagonal + 2.0 * mixed)
            high = field.astype(jnp.bfloat16)
            low = (field - high.astype(jnp.float32)).astype(jnp.bfloat16)
            rows = pl.ds(pl.multiple_of(96 * k + row, 16), 16)
            q_terms[rows, 0:128] = high
            q_terms[rows, 128:256] = low
            for c in range(2):
                flat[96 * c + row : 96 * c + row + 16, :] += weight[c] * field
        return carry

    lax.fori_loop(0, 16, plane, 0, unroll=4)

    for copy in weight_copies:
        copy.wait()
    wx[0:128, :] = wx_held[...].astype(jnp.float32).astype(jnp.bfloat16)
    wx[128:256, :] = wx_held[...].astype(jnp.float32).astype(jnp.bfloat16)
    phx[:, 0:128] = px_held[...].astype(jnp.float32).astype(jnp.bfloat16)
    phx[:, 128:256] = px_held[...].astype(jnp.float32).astype(jnp.bfloat16)
    wy = wy_held[...].astype(jnp.float32)
    wz = wz_held[...].astype(jnp.float32)

    flat_high = flat[...].astype(jnp.bfloat16)
    flat_terms[:, 0:128] = flat_high
    flat_terms[:, 128:256] = (flat[...] - flat_high.astype(jnp.float32)).astype(jnp.bfloat16)
    leading = lax.dot_general(
        phx[...], flat_terms[...], (((1,), (1,)), ((), ())), preferred_element_type=jnp.float32
    )
    lead[0] = leading[:, 0:128]
    lead[1] = leading[:, 128:256]

    total_y = jnp.zeros((96, 256), jnp.float32)
    for k in range(16):
        rows = slice(96 * k, 96 * k + 96)
        sums = jnp.dot(q_terms[rows, :], wx[...], preferred_element_type=jnp.float32)
        total_y = total_y + sums * wz[k : k + 1, :]
        part_z[k : k + 1, :] = jnp.sum(sums * wy, axis=0, keepdims=True)
        wyz[rows, :] = (wy * wz[k : k + 1, :]).astype(jnp.bfloat16)
    part_y[...] = total_y

    lane8 = lax.broadcasted_iota(jnp.int32, (8, 128), 1)
    for g in range(16):
        for z in range(2):
            chunk = 2 * g + z
            base = 40 * chunk
            near = 32 * g + z
            send[base : base + 16, :] = lead[0, pl.ds(near, 16, stride=2), :]
            send[base + 16 : base + 24, :] = jnp.where(
                lane8 < 64,
                lead[1, pl.ds(near, 8, stride=2), :],
                pltpu.roll(lead[1, pl.ds(near + 16, 8, stride=2), :], 64, 1),
            )
            rank = 4 * ((g // 4) % 2) + g % 4
            spot = 6 * (2 * rank + z)
            for half in range(2):
                lanes = slice(128 * half, 128 * half + 128)
                send[base + 24 + 6 * half : base + 30 + 6 * half, :] = part_y[spot : spot + 6, lanes]
                send[base + 36 + 2 * half : base + 38 + 2 * half, :] = part_z[2 * rank : 2 * rank + 2, lanes]

    turned = lax.dot_general(
        q_terms[...], wyz[...], (((0,), (0,)), ((), ())), preferred_element_type=jnp.float32
    )
    turned = turned[0:128, :] + turned[128:256, :]
    for h in range(16):
        part_x[16 * h : 16 * h + 8, :] = turned[8 * h : 8 * h + 8, 0:128]
        part_x[16 * h + 8 : 16 * h + 16, :] = turned[8 * h : 8 * h + 8, 128:256]


def field(velocity, far, below, above, sides, omega_x, omega_y, omega_z, phi_x, phi_z):
    whole = pl.BlockSpec(memory_space=pltpu.VMEM)
    outside = pl.BlockSpec(memory_space=pl.ANY)
    return pl.pallas_call(
        field_kernel,
        in_specs=[outside] * 13,
        out_specs=[whole] * 2,
        out_shape=[jax.ShapeDtypeStruct((1280, 128), jnp.float32), jax.ShapeDtypeStruct((256, 128), jnp.float32)],
        scratch_shapes=[
            pltpu.VMEM((3, 20, 112, 128), jnp.float32),
            pltpu.VMEM((3, 16, 96, 128), jnp.float32),
            pltpu.VMEM((2, 96, 128), jnp.float32),
            pltpu.VMEM((2, 3, 32, 128), jnp.float32),
            pltpu.VMEM((128, 256), jnp.int32),
            pltpu.VMEM((96, 256), jnp.int32),
            pltpu.VMEM((16, 256), jnp.int32),
            pltpu.VMEM((512, 128), jnp.int32),
            pltpu.VMEM((1536, 256), jnp.bfloat16),
            pltpu.VMEM((256, 128), jnp.float32),
            pltpu.VMEM((256, 256), jnp.bfloat16),
            pltpu.VMEM((256, 256), jnp.bfloat16),
            pltpu.VMEM((1536, 256), jnp.bfloat16),
            pltpu.VMEM((512, 256), jnp.bfloat16),
            pltpu.VMEM((96, 256), jnp.float32),
            pltpu.VMEM((16, 256), jnp.float32),
            pltpu.VMEM((2, 512, 128), jnp.float32),
            pltpu.SMEM((2, 16), jnp.int32),
            pltpu.SemaphoreType.DMA((14,)),
        ],
        compiler_params=pltpu.CompilerParams(vmem_limit_bytes=32 * 1024 * 1024),
        name="field_products",
    )(velocity, far, below, above, *sides, omega_x, omega_y, omega_z, phi_x, phi_z)


def split(values):
    high = lax.reduce_precision(values, 8, 7)
    return high.astype(jnp.bfloat16), (values - high).astype(jnp.bfloat16)


NEAR = [[4 * x + r for r in range(4)] for x in range(4)]


def gather(rows):
    return lax.all_gather(rows, "gx", axis=0, tiled=True, axis_index_groups=NEAR)


def pair_swap(rows):
    return lax.ppermute(rows, "gx", [(i, i ^ 4) for i in range(16)])


def unfold_kernel(own, beside, factor_y, factor_z):
    scale_y = 1.0 / math.sqrt(2048 * 32)
    scale_z = 1.0 / math.sqrt(2048 * 1536)
    gz = lax.axis_index("gz")
    pair = lax.rem(lax.axis_index("gx") // 4, 2)
    for x in range(2):
        rows_z = jnp.where(pair == x, own[96:112, :], beside[96:112, :]) * scale_z
        for z in range(2):
            near = jnp.where(gz == z, own[0:48, :], own[48:96, :])
            away = jnp.where(gz == z, beside[0:48, :], beside[48:96, :])
            rows_y = jnp.where(pair == x, near, away) * scale_y
            for r in range(4):
                rank = 4 * x + r
                spot = 6 * (2 * rank + z)
                factor_y[spot : spot + 6, 0:128] = rows_y[12 * r : 12 * r + 6, :]
                factor_y[spot : spot + 6, 128:256] = rows_y[12 * r + 6 : 12 * r + 12, :]
        for r in range(4):
            rank = 4 * x + r
            factor_z[2 * rank : 2 * rank + 2, 0:128] = rows_z[4 * r : 4 * r + 2, :]
            factor_z[2 * rank : 2 * rank + 2, 128:256] = rows_z[4 * r + 2 : 4 * r + 4, :]


def unfold(*pieces):
    whole = pl.BlockSpec(memory_space=pltpu.VMEM)
    return pl.pallas_call(
        unfold_kernel,
        in_specs=[whole] * 2,
        out_specs=[whole] * 2,
        out_shape=[jax.ShapeDtypeStruct((96, 256), jnp.float32), jax.ShapeDtypeStruct((16, 256), jnp.float32)],
        compiler_params=pltpu.CompilerParams(vmem_limit_bytes=4 * 1024 * 1024),
        cost_estimate=pl.CostEstimate(flops=0, bytes_accessed=0, transcendentals=0),
        name="unfold_factors",
    )(*pieces)


def exchange(rows, axes):
    return lax.all_to_all(rows, axes, 0, 0, tiled=True)


def shards(velocity, below, above, omega_x, omega_y, omega_z, phi_x, phi_y, phi_z):
    total_x = 2048
    total_y = 1536
    total_z = 32
    gz = lax.axis_index("gz")
    near, x_even, x_odd, y_even, y_odd = pack(velocity)
    far = shift_permute(near, "gz", 1)
    y_even = edge_swap(y_even, "gy", 0)
    y_odd = edge_swap(y_odd, "gy", 1)
    x_odd = edge_swap(x_odd, "gx", 1)
    x_even = edge_swap(x_even, "gx", 0)
    sides = [y_even, y_odd, x_odd, x_even]
    send, part_x = field(velocity, far, below, above, sides, omega_x, omega_y, omega_z, phi_x, phi_z)
    got = exchange(send, ("gx", "gz")).reshape(16, 2, 40, 128)
    part_x = part_x + shift_permute(part_x, "gz", 1)

    by_z = jnp.sum(got, axis=0)
    summed = by_z[0] + by_z[1]
    summed_z = jnp.where(gz == 0, by_z[0, 36:40], by_z[1, 36:40])
    rest = jnp.concatenate([summed[16:24, :64], summed[16:24, 64:]], axis=0)
    lead_high, lead_low = split(jnp.concatenate([summed[:16], rest], axis=1))
    wide = phi_y.T.astype(jnp.bfloat16)
    none = jnp.zeros((96, 512), jnp.bfloat16)
    wide = jnp.concatenate(
        [jnp.concatenate([wide, none], axis=1), jnp.concatenate([none, wide], axis=1)], axis=0
    )
    core = jnp.dot(jnp.concatenate([lead_high, lead_low], axis=0), wide, preferred_element_type=jnp.float32)
    core = (core[:16] + core[16:]).reshape(16, 8, 128)
    rows_z = jnp.broadcast_to(summed_z[None], (16, 4, 128))
    send = jnp.concatenate([core, part_x.reshape(16, 16, 128), rows_z], axis=1)
    got = jnp.sum(exchange(send.reshape(16, 7, 4, 128), "gy"), axis=0).reshape(28, 128)
    core_sketch = got[:8].reshape(1, 2, 512) * (1.0 / math.sqrt(total_x * total_y * total_z))

    own_y = gather(summed[24:36])
    both_y = jnp.concatenate([own_y, shift_permute(own_y, "gz", 1)], axis=0)
    rows, both_y = lax.optimization_barrier((got[8:28], both_y))
    got_x = exchange(jnp.broadcast_to(rows[None, :16], (16, 16, 128)).reshape(256, 128), "gy")
    own = jnp.concatenate([both_y, gather(rows[16:])], axis=0)
    factor_y, factor_z = unfold(own, pair_swap(own))

    factor_x = got_x.reshape(16, 2, 8, 128).transpose(0, 2, 1, 3).reshape(128, 256)
    factor_x = factor_x * (1.0 / math.sqrt(total_y * total_z))
    return (factor_x, factor_y, factor_z, core_sketch)


def solution(mesh):
    in_specs = (
        P(None, "gz", "gy", "gx"),
        P(None, None, "gy", "gx"),
        P(None, None, "gy", "gx"),
        P("gx", None),
        P("gy", None),
        P("gz", None),
        P(None, "gx"),
        P(None, "gy"),
        P(None, "gz"),
    )
    out_specs = (P("gx", None), P("gy", None), P("gz", None), P(("gx", "gy", "gz"), None, None))
    return jax.shard_map(shards, mesh=mesh, in_specs=in_specs, out_specs=out_specs, check_vma=False)
```

```python
import math

import jax
import jax.numpy as jnp
from jax import lax
from jax.experimental import pallas as pl
from jax.experimental.pallas import tpu as pltpu
from jax.sharding import PartitionSpec as P


def shift_permute(cells, axis, step):
    count = lax.axis_size(axis)
    return lax.ppermute(cells, axis, [(i, (i + step) % count) for i in range(count)])


def edge_swap(cells, axis, odd):
    count = lax.axis_size(axis)
    pairs = []
    for i in range(odd, count + odd, 2):
        pairs += [(i % count, (i + 1) % count), ((i + 1) % count, i % count)]
    return lax.ppermute(cells, axis, pairs)


def rims_kernel(vel, near, y_even, y_odd, head, tail, sems):
    gz = lax.axis_index("gz")
    odd_y = lax.rem(lax.axis_index("gy"), 2) == 1
    copies = [
        pltpu.make_async_copy(vel.at[:, pl.ds(14 * (1 - gz), 2)], near, sems.at[0]),
        pltpu.make_async_copy(vel.at[:, :, pl.ds(0, 8), :], head, sems.at[1]),
        pltpu.make_async_copy(vel.at[:, :, pl.ds(88, 8), :], tail, sems.at[2]),
    ]
    for copy in copies:
        copy.start()
    for copy in copies:
        copy.wait()
    for c in range(3):
        for k in range(16):
            first = head[c, k, 0:2, :]
            last = tail[c, k, 6:8, :]
            y_even[c, 2 * k : 2 * k + 2, :] = jnp.where(odd_y, first, last)
            y_odd[c, 2 * k : 2 * k + 2, :] = jnp.where(odd_y, last, first)


def pack_kernel(vel, x_even, x_odd):
    odd_x = lax.rem(lax.axis_index("gx"), 2) == 1
    lane = lax.broadcasted_iota(jnp.int32, (96, 128), 1)
    high = jnp.zeros((96, 128), jnp.float32)
    low = jnp.zeros((96, 128), jnp.float32)
    for c in range(3):
        for k in range(16):
            spot = 2 * (16 * c + k)
            turned = pltpu.roll(vel[c, k], spot + 2, 1)
            high = jnp.where((lane >= spot) & (lane < spot + 2), turned, high)
            low = jnp.where((lane >= spot + 2) & (lane < spot + 4), turned, low)
    x_even[...] = jnp.where(odd_x, low, high)
    x_odd[...] = jnp.where(odd_x, high, low)


def pack(velocity):
    rims = jax.ShapeDtypeStruct((96, 128), jnp.float32)
    rows = jax.ShapeDtypeStruct((3, 32, 128), jnp.float32)
    whole = pl.BlockSpec(memory_space=pltpu.VMEM)
    near, y_even, y_odd = pl.pallas_call(
        rims_kernel,
        in_specs=[pl.BlockSpec(memory_space=pl.ANY)],
        out_specs=[whole] * 3,
        out_shape=[jax.ShapeDtypeStruct((3, 2, 96, 128), jnp.float32), rows, rows],
        scratch_shapes=[
            pltpu.VMEM((3, 16, 8, 128), jnp.float32),
            pltpu.VMEM((3, 16, 8, 128), jnp.float32),
            pltpu.SemaphoreType.DMA((3,)),
        ],
        compiler_params=pltpu.CompilerParams(vmem_limit_bytes=62 * 1024 * 1024),
        name="pack_rims",
    )(velocity)
    x_even, x_odd = pl.pallas_call(
        pack_kernel,
        in_specs=[whole],
        out_specs=[whole] * 2,
        out_shape=[rims, rims],
        compiler_params=pltpu.CompilerParams(vmem_limit_bytes=32 * 1024 * 1024),
        name="pack_halos",
    )(velocity)
    return near, x_even, x_odd, y_even, y_odd


def field_kernel(
    vel, far, below, above, y_even, y_odd, x_odd, x_even, omega_x, omega_y, omega_z, phi_x, phi_z,
    send, part_x,
    padded, sides, x_held, y_held, wx_held, wy_held, wz_held, px_held,
    q_terms, flat, flat_terms, wx, wyz, phx, part_y, part_z, lead, pz_held, sems,
):
    gz = lax.axis_index("gz")
    odd_x = lax.rem(lax.axis_index("gx"), 2)
    odd_y = lax.rem(lax.axis_index("gy"), 2)
    middle = pl.ds(8, 96)
    x_copies = [
        pltpu.make_async_copy(x_even, x_held.at[1 - odd_x], sems.at[0]),
        pltpu.make_async_copy(x_odd, x_held.at[odd_x], sems.at[1]),
    ]
    y_copies = [
        pltpu.make_async_copy(y_even, y_held.at[1 - odd_y], sems.at[2]),
        pltpu.make_async_copy(y_odd, y_held.at[odd_y], sems.at[3]),
    ]
    cells_copies = [
        pltpu.make_async_copy(vel.at[c], padded.at[c, pl.ds(2, 16), middle, :], sems.at[4 + c]) for c in range(3)
    ]
    far_low = pltpu.make_async_copy(far, padded.at[:, pl.ds(0, 2), middle, :], sems.at[7])
    far_high = pltpu.make_async_copy(far, padded.at[:, pl.ds(18, 2), middle, :], sems.at[8])
    rim_low = pltpu.make_async_copy(below, padded.at[:, pl.ds(0, 2), middle, :], sems.at[7])
    rim_high = pltpu.make_async_copy(above, padded.at[:, pl.ds(18, 2), middle, :], sems.at[8])
    weight_copies = [
        pltpu.make_async_copy(omega_x, wx_held, sems.at[9]),
        pltpu.make_async_copy(omega_y, wy_held, sems.at[10]),
        pltpu.make_async_copy(omega_z, wz_held, sems.at[11]),
        pltpu.make_async_copy(phi_x, px_held, sems.at[12]),
    ]
    z_copy = pltpu.make_async_copy(phi_z, pz_held, sems.at[13])
    for copy in x_copies + cells_copies + y_copies + [z_copy]:
        copy.start()

    @pl.when(gz == 0)
    def _():
        rim_low.start()
        far_high.start()

    @pl.when(gz == 1)
    def _():
        far_low.start()
        rim_high.start()

    for copy in weight_copies:
        copy.start()
    for copy in x_copies:
        copy.wait()

    lane_all = lax.broadcasted_iota(jnp.int32, (96, 128), 1)

    def place(k, carry):
        for c in range(3):
            spot = 2 * (16 * c + k)
            both = jnp.where(lane_all < spot + 2, x_held[0], x_held[1])
            sides[c, k] = pltpu.roll(both, 126 - spot, 1)
        return carry

    lax.fori_loop(0, 16, place, 0, unroll=2)

    for copy in y_copies + cells_copies + [z_copy]:
        copy.wait()
    for c in range(3):
        for k in range(16):
            padded[c, k + 2, 6:8, :] = y_held[0, c, 2 * k : 2 * k + 2, :]
            padded[c, k + 2, 104:106, :] = y_held[1, c, 2 * k : 2 * k + 2, :]
    flat[...] = jnp.zeros((256, 128), jnp.float32)

    @pl.when(gz == 0)
    def _():
        rim_low.wait()
        far_high.wait()

    @pl.when(gz == 1)
    def _():
        far_low.wait()
        rim_high.wait()

    lane = lax.broadcasted_iota(jnp.int32, (16, 128), 1)

    def plane(k, carry):
        weight = [pz_held[c, k].astype(jnp.float32) for c in range(2)]
        for block in range(6):
            row = 16 * block
            at = row + 8
            along = [[], [], []]
            for c in range(3):
                cells = padded[c, k + 2, at : at + 16, :]
                rim = sides[c, k, row : row + 16, :]
                outer = pltpu.roll(jnp.where(lane >= 126, rim, cells), 2, 1) - pltpu.roll(
                    jnp.where(lane < 2, rim, cells), 126, 1
                )
                inner = pltpu.roll(jnp.where(lane < 1, rim, cells), 127, 1) - pltpu.roll(
                    jnp.where(lane >= 127, rim, cells), 1, 1
                )
                along[0].append(outer + 8.0 * inner)
                outer = padded[c, k + 2, at - 2 : at + 14, :] - padded[c, k + 2, at + 2 : at + 18, :]
                inner = padded[c, k + 2, at + 1 : at + 17, :] - padded[c, k + 2, at - 1 : at + 15, :]
                along[1].append(outer + 8.0 * inner)
                outer = padded[c, k, at : at + 16, :] - padded[c, k + 4, at : at + 16, :]
                inner = padded[c, k + 3, at : at + 16, :] - padded[c, k + 1, at : at + 16, :]
                along[2].append(outer + 8.0 * inner)
            diagonal = along[0][0] * along[0][0] + along[1][1] * along[1][1] + along[2][2] * along[2][2]
            mixed = along[0][1] * along[1][0] + along[0][2] * along[2][0] + along[1][2] * along[2][1]
            field = (-0.5 / 144.0) * (diagonal + 2.0 * mixed)
            high = field.astype(jnp.bfloat16)
            low = (field - high.astype(jnp.float32)).astype(jnp.bfloat16)
            rows = pl.ds(pl.multiple_of(96 * k + row, 16), 16)
            q_terms[rows, 0:128] = high
            q_terms[rows, 128:256] = low
            for c in range(2):
                flat[96 * c + row : 96 * c + row + 16, :] += weight[c] * field
        return carry

    lax.fori_loop(0, 16, plane, 0, unroll=4)

    for copy in weight_copies:
        copy.wait()
    wx[0:128, :] = wx_held[...].astype(jnp.float32).astype(jnp.bfloat16)
    wx[128:256, :] = wx_held[...].astype(jnp.float32).astype(jnp.bfloat16)
    phx[:, 0:128] = px_held[...].astype(jnp.float32).astype(jnp.bfloat16)
    phx[:, 128:256] = px_held[...].astype(jnp.float32).astype(jnp.bfloat16)
    wy = wy_held[...].astype(jnp.float32)
    wz = wz_held[...].astype(jnp.float32)

    flat_high = flat[...].astype(jnp.bfloat16)
    flat_terms[:, 0:128] = flat_high
    flat_terms[:, 128:256] = (flat[...] - flat_high.astype(jnp.float32)).astype(jnp.bfloat16)
    leading = lax.dot_general(
        phx[...], flat_terms[...], (((1,), (1,)), ((), ())), preferred_element_type=jnp.float32
    )
    lead[0] = leading[:, 0:128]
    lead[1] = leading[:, 128:256]

    total_y = jnp.zeros((96, 256), jnp.float32)
    for k in range(16):
        rows = slice(96 * k, 96 * k + 96)
        sums = jnp.dot(q_terms[rows, :], wx[...], preferred_element_type=jnp.float32)
        total_y = total_y + sums * wz[k : k + 1, :]
        part_z[k : k + 1, :] = jnp.sum(sums * wy, axis=0, keepdims=True)
        wyz[rows, :] = (wy * wz[k : k + 1, :]).astype(jnp.bfloat16)
    part_y[...] = total_y

    lane8 = lax.broadcasted_iota(jnp.int32, (8, 128), 1)
    for g in range(16):
        for z in range(2):
            chunk = 2 * g + z
            base = 40 * chunk
            near = 32 * g + z
            send[base : base + 16, :] = lead[0, pl.ds(near, 16, stride=2), :]
            send[base + 16 : base + 24, :] = jnp.where(
                lane8 < 64,
                lead[1, pl.ds(near, 8, stride=2), :],
                pltpu.roll(lead[1, pl.ds(near + 16, 8, stride=2), :], 64, 1),
            )
            rank = 4 * ((g // 4) % 2) + g % 4
            spot = 6 * (2 * rank + z)
            for half in range(2):
                lanes = slice(128 * half, 128 * half + 128)
                send[base + 24 + 6 * half : base + 30 + 6 * half, :] = part_y[spot : spot + 6, lanes]
                send[base + 36 + 2 * half : base + 38 + 2 * half, :] = part_z[2 * rank : 2 * rank + 2, lanes]

    turned = lax.dot_general(
        q_terms[...], wyz[...], (((0,), (0,)), ((), ())), preferred_element_type=jnp.float32
    )
    turned = turned[0:128, :] + turned[128:256, :]
    for h in range(16):
        part_x[16 * h : 16 * h + 8, :] = turned[8 * h : 8 * h + 8, 0:128]
        part_x[16 * h + 8 : 16 * h + 16, :] = turned[8 * h : 8 * h + 8, 128:256]


def field(velocity, far, below, above, sides, omega_x, omega_y, omega_z, phi_x, phi_z):
    whole = pl.BlockSpec(memory_space=pltpu.VMEM)
    outside = pl.BlockSpec(memory_space=pl.ANY)
    return pl.pallas_call(
        field_kernel,
        in_specs=[outside] * 13,
        out_specs=[whole] * 2,
        out_shape=[jax.ShapeDtypeStruct((1280, 128), jnp.float32), jax.ShapeDtypeStruct((256, 128), jnp.float32)],
        scratch_shapes=[
            pltpu.VMEM((3, 20, 112, 128), jnp.float32),
            pltpu.VMEM((3, 16, 96, 128), jnp.float32),
            pltpu.VMEM((2, 96, 128), jnp.float32),
            pltpu.VMEM((2, 3, 32, 128), jnp.float32),
            pltpu.VMEM((128, 256), jnp.int32),
            pltpu.VMEM((96, 256), jnp.int32),
            pltpu.VMEM((16, 256), jnp.int32),
            pltpu.VMEM((512, 128), jnp.int32),
            pltpu.VMEM((1536, 256), jnp.bfloat16),
            pltpu.VMEM((256, 128), jnp.float32),
            pltpu.VMEM((256, 256), jnp.bfloat16),
            pltpu.VMEM((256, 256), jnp.bfloat16),
            pltpu.VMEM((1536, 256), jnp.bfloat16),
            pltpu.VMEM((512, 256), jnp.bfloat16),
            pltpu.VMEM((96, 256), jnp.float32),
            pltpu.VMEM((16, 256), jnp.float32),
            pltpu.VMEM((2, 512, 128), jnp.float32),
            pltpu.SMEM((2, 16), jnp.int32),
            pltpu.SemaphoreType.DMA((14,)),
        ],
        compiler_params=pltpu.CompilerParams(vmem_limit_bytes=32 * 1024 * 1024),
        name="field_products",
    )(velocity, far, below, above, *sides, omega_x, omega_y, omega_z, phi_x, phi_z)


def split(values):
    high = lax.reduce_precision(values, 8, 7)
    return high.astype(jnp.bfloat16), (values - high).astype(jnp.bfloat16)


NEAR = [[4 * x + r for r in range(4)] for x in range(4)]


def gather(rows):
    return lax.all_gather(rows, "gx", axis=0, tiled=True, axis_index_groups=NEAR)


def pair_swap(rows):
    return lax.ppermute(rows, "gx", [(i, i ^ 4) for i in range(16)])


def unfold_kernel(own, beside, factor_y, factor_z):
    scale_y = 1.0 / math.sqrt(2048 * 32)
    scale_z = 1.0 / math.sqrt(2048 * 1536)
    gz = lax.axis_index("gz")
    pair = lax.rem(lax.axis_index("gx") // 4, 2)
    for x in range(2):
        rows_z = jnp.where(pair == x, own[96:112, :], beside[96:112, :]) * scale_z
        for z in range(2):
            near = jnp.where(gz == z, own[0:48, :], own[48:96, :])
            away = jnp.where(gz == z, beside[0:48, :], beside[48:96, :])
            rows_y = jnp.where(pair == x, near, away) * scale_y
            for r in range(4):
                rank = 4 * x + r
                spot = 6 * (2 * rank + z)
                factor_y[spot : spot + 6, 0:128] = rows_y[12 * r : 12 * r + 6, :]
                factor_y[spot : spot + 6, 128:256] = rows_y[12 * r + 6 : 12 * r + 12, :]
        for r in range(4):
            rank = 4 * x + r
            factor_z[2 * rank : 2 * rank + 2, 0:128] = rows_z[4 * r : 4 * r + 2, :]
            factor_z[2 * rank : 2 * rank + 2, 128:256] = rows_z[4 * r + 2 : 4 * r + 4, :]


def unfold(*pieces):
    whole = pl.BlockSpec(memory_space=pltpu.VMEM)
    return pl.pallas_call(
        unfold_kernel,
        in_specs=[whole] * 2,
        out_specs=[whole] * 2,
        out_shape=[jax.ShapeDtypeStruct((96, 256), jnp.float32), jax.ShapeDtypeStruct((16, 256), jnp.float32)],
        compiler_params=pltpu.CompilerParams(vmem_limit_bytes=4 * 1024 * 1024),
        cost_estimate=pl.CostEstimate(flops=0, bytes_accessed=0, transcendentals=0),
        name="unfold_factors",
    )(*pieces)


def exchange(rows, axes):
    return lax.all_to_all(rows, axes, 0, 0, tiled=True)


def shards(velocity, below, above, omega_x, omega_y, omega_z, phi_x, phi_y, phi_z):
    total_x = 2048
    total_y = 1536
    total_z = 32
    gz = lax.axis_index("gz")
    near, x_even, x_odd, y_even, y_odd = pack(velocity)
    far = shift_permute(near, "gz", 1)
    y_even = edge_swap(y_even, "gy", 0)
    y_odd = edge_swap(y_odd, "gy", 1)
    x_odd = edge_swap(x_odd, "gx", 1)
    x_even = edge_swap(x_even, "gx", 0)
    sides = [y_even, y_odd, x_odd, x_even]
    send, part_x = field(velocity, far, below, above, sides, omega_x, omega_y, omega_z, phi_x, phi_z)
    got = exchange(send, ("gx", "gz")).reshape(16, 2, 40, 128)
    part_x = part_x + shift_permute(part_x, "gz", 1)

    by_z = jnp.sum(got, axis=0)
    summed = by_z[0] + by_z[1]
    summed_z = jnp.where(gz == 0, by_z[0, 36:40], by_z[1, 36:40])
    rest = jnp.concatenate([summed[16:24, :64], summed[16:24, 64:]], axis=0)
    lead_high, lead_low = split(jnp.concatenate([summed[:16], rest], axis=1))
    wide = phi_y.T.astype(jnp.bfloat16)
    none = jnp.zeros((96, 512), jnp.bfloat16)
    wide = jnp.concatenate(
        [jnp.concatenate([wide, none], axis=1), jnp.concatenate([none, wide], axis=1)], axis=0
    )
    core = jnp.dot(jnp.concatenate([lead_high, lead_low], axis=0), wide, preferred_element_type=jnp.float32)
    core = (core[:16] + core[16:]).reshape(16, 8, 128)
    rows_z = jnp.broadcast_to(summed_z[None], (16, 4, 128))
    send = jnp.concatenate([core, part_x.reshape(16, 16, 128), rows_z], axis=1)
    got = jnp.sum(exchange(send.reshape(16, 7, 4, 128), "gy"), axis=0).reshape(28, 128)
    core_sketch = got[:8].reshape(1, 2, 512) * (1.0 / math.sqrt(total_x * total_y * total_z))

    own_y = gather(summed[24:36])
    both_y = jnp.concatenate([own_y, shift_permute(own_y, "gz", 1)], axis=0)
    rows, both_y = lax.optimization_barrier((got[8:28], both_y))
    got_x = exchange(jnp.broadcast_to(rows[None, :16], (16, 16, 128)).reshape(256, 128), "gy")
    own = jnp.concatenate([both_y, gather(rows[16:])], axis=0)
    factor_y, factor_z = unfold(own, pair_swap(own))

    factor_x = got_x.reshape(16, 2, 8, 128).transpose(0, 2, 1, 3).reshape(128, 256)
    factor_x = factor_x * (1.0 / math.sqrt(total_y * total_z))
    return (factor_x, factor_y, factor_z, core_sketch)


def solution(mesh):
    in_specs = (
        P(None, "gz", "gy", "gx"),
        P(None, None, "gy", "gx"),
        P(None, None, "gy", "gx"),
        P("gx", None),
        P("gy", None),
        P("gz", None),
        P(None, "gx"),
        P(None, "gy"),
        P(None, "gz"),
    )
    out_specs = (P("gx", None), P("gy", None), P("gz", None), P(("gx", "gy", "gz"), None, None))
    return jax.shard_map(shards, mesh=mesh, in_specs=in_specs, out_specs=out_specs, check_vma=False)
```
